128 devices in a mesh: layer: 2 (over core), row: 4 (over x), col: 16 (over z, y).
Axes of the slice: x: 4, y: 4, z: 4, core: 2. Of those that a mesh axis runs over, the one named last changes fastest.
Arguments:
- hamiltonian: bfloat16 [8, 16, 23, 128, 128], P(('layer', 'row'), 'col'), may hold values from -3 to 3
- cheb_low: bfloat16 [8, 16, 23, 128, 128], P(('layer', 'row'), 'col'), may hold values from -1.25 to 1.25
- cheb_high: bfloat16 [8, 16, 23, 128, 128], P(('layer', 'row'), 'col'), may hold values from -1.25 to 1.25
- pattern: int32 [2, 4, 16, 2, 23], P(None, 'row', 'col'), may hold values from -1 to 95, as said below
- atoms: int32 [768], P(('layer', 'row')), may hold values from 8 to 16
Outputs:
- cheb_even: bfloat16 [8, 16, 23, 128, 128], P(('layer', 'row'), 'col')
- cheb_odd: bfloat16 [8, 16, 23, 128, 128], P(('layer', 'row'), 'col')
The draws below stay inside these ranges and needn't reach their ends.
Inputs may be any that keep to these rules, and one draw needn't show every extreme that they name: `pattern`: entry [q, r, g, 0, t] is a block row of the piece (below 96) and entry [q, r, g, 1, t] a block column of the group (below 48), both -1 in an empty slot. The live blocks of one piece and group are distinct, and no two of them share a block row. In every draw some piece-group pairs fill all 23 slots.
All inputs are finite; a program needn't handle non-finite values.
Results may differ from the reference program's by a relative error of at most 0.011.
Values may be sent and summed in bfloat16 or wider, within the bound.
No kernel may reach another device: no remote copies, remote signals or barrier semaphores. Data moves between devices by JAX's collectives and lax.ppermute only.
A program may use at most 192 MiB of HBM per device.

```python
import jax
import jax.numpy as jnp
from jax import lax

TILE = 128
RB = 96
CAP = 23
FUNCS = 8
LAYERS = 2
ROWGROUPS = 4
GROUPS = 16
PIECES = 8
SPREAD = 4
SUBROWS = 24
NB = 768
WIDTH = 48
SK = 1


def distinct_order(key, out_shape, extent):
    scores = jax.random.randint(key, out_shape, 0, 1 << 20) * extent + jnp.arange(extent, dtype=jnp.int32)
    return jnp.argsort(scores, axis=-1).astype(jnp.int32)


def draw_pattern(key, part):
    key = jax.random.fold_in(key, 7)
    subkeys = jax.random.split(key, 5)
    pieces = jnp.arange(PIECES, dtype=jnp.int32)[:, None]
    column_groups = jnp.arange(GROUPS, dtype=jnp.int32)[None, :]
    central = pieces % ROWGROUPS == column_groups // SPREAD
    counts = jax.random.randint(subkeys[0], (PIECES, GROUPS), CAP // 4, 3 * CAP // 4 + 1)
    counts = jnp.where(central, CAP, counts)
    local_rows = jnp.arange(RB, dtype=jnp.int32)[None, None, :]
    diag_row = central[:, :, None] & (local_rows // SUBROWS == column_groups[:, :, None] % SPREAD)
    row_scores = jax.random.randint(subkeys[1], (PIECES, GROUPS, RB), 0, 1 << 20) * RB + local_rows
    row_scores = row_scores - diag_row.astype(jnp.int32) * (1 << 28)
    row_order = jnp.argsort(row_scores, axis=-1).astype(jnp.int32)
    slot_ids = jnp.arange(CAP, dtype=jnp.int32)
    row_of = jnp.take_along_axis(row_order, jnp.broadcast_to(slot_ids % RB, (PIECES, GROUPS, CAP)), axis=2)
    slot_rank = slot_ids // RB
    diag_col = pieces[:, :, None] // ROWGROUPS * SUBROWS + local_rows % SUBROWS
    base_col = jnp.where(diag_row, diag_col, jax.random.randint(subkeys[2], (PIECES, GROUPS, RB), 0, WIDTH))
    col_steps = distinct_order(subkeys[3], (PIECES, GROUPS, RB, WIDTH - 1), WIDTH - 1)[..., :SK - 1] + 1
    shifts = jnp.concatenate([jnp.zeros((PIECES, GROUPS, RB, 1), jnp.int32), col_steps], axis=3)
    shifts = shifts.reshape(PIECES, GROUPS, RB * SK)
    shift_of = jnp.take_along_axis(shifts, row_of * SK + slot_rank[None, None, :], axis=2)
    col_of = (jnp.take_along_axis(base_col, row_of, axis=2) + shift_of) % WIDTH
    is_live = slot_ids[None, None, :] < counts[:, :, None]
    live_rows = jnp.where(is_live, row_of, -1)
    live_cols = jnp.where(is_live, col_of, -1)
    shuffle = distinct_order(subkeys[4], (PIECES, GROUPS, CAP), CAP)
    live_rows = jnp.take_along_axis(live_rows, shuffle, axis=2)
    live_cols = jnp.take_along_axis(live_cols, shuffle, axis=2)
    stacked = jnp.stack([live_rows, live_cols], axis=2)
    return stacked.reshape(LAYERS, ROWGROUPS, GROUPS, 2, CAP).astype(jnp.int32)


def touch_ends(entries, key, smallest, high):
    spot = [jax.random.randint(jax.random.fold_in(key, axis), (), 0, length) for axis, length in enumerate(entries.shape)]
    longest = entries.shape.index(max(entries.shape))
    beside = spot[:longest] + [(spot[longest] + 1) % entries.shape[longest]] + spot[longest + 1:]
    return entries.at[tuple(spot)].set(smallest).at[tuple(beside)].set(high)


def shard_levels(stream_key, shape, cuts, least, high):
    factor_of = 1.0
    for position, blocks in cuts:
        draws = jax.random.uniform(jax.random.fold_in(jax.random.fold_in(stream_key, 6), position), (blocks,), jnp.float32, least / len(cuts), high / len(cuts))
        factor_of = factor_of * jnp.repeat(jnp.exp(draws), shape[position] // blocks).reshape((-1,) + (1,) * (len(shape) - 1 - position))
    return factor_of


def scatter_about(rng, shape, spread, reach, shards=(), kind=jnp.bfloat16):
    factor_of = shard_levels(rng, shape, shards, -0.22, 0.18) if shards else 1.0
    drawn = jax.random.normal(rng, shape, jnp.float32) * spread * factor_of
    return jnp.minimum(jnp.maximum(drawn, -reach), reach).astype(kind)


def setup_inputs(seed: int = 0) -> dict:
    keys = jax.random.split(jax.random.key(seed), 6)
    return {
        "hamiltonian": scatter_about(keys[0], (PIECES, GROUPS, CAP, TILE, TILE), 0.5, 3.0, ((0, 8), (1, 16))),
        "cheb_low": scatter_about(keys[1], (PIECES, GROUPS, CAP, TILE, TILE), 0.2, 1.25, ((0, 8), (1, 16))),
        "cheb_high": scatter_about(keys[2], (PIECES, GROUPS, CAP, TILE, TILE), 0.2, 1.25, ((0, 8), (1, 16))),
        "pattern": draw_pattern(jax.random.fold_in(keys[5], 71), 0),
        "atoms": touch_ends(jax.random.randint(keys[4], (NB,), TILE // (2 * FUNCS), TILE // FUNCS + 1), jax.random.fold_in(keys[4], 1), TILE // (2 * FUNCS), (TILE // FUNCS + 1) - 1).astype(jnp.int32),
    }


def block_column(group_id, local_col):
    return ((local_col // SUBROWS) * ROWGROUPS + group_id // SPREAD) * RB + (group_id % SPREAD) * SUBROWS + local_col % SUBROWS


def rank_in_row(row_ids):
    earlier = jnp.arange(row_ids.shape[-1], dtype=jnp.int32)
    matches = (row_ids[..., :, None] == row_ids[..., None, :]) & (earlier[None, :] < earlier[:, None])
    return jnp.sum(matches.astype(jnp.int32), axis=-1)


def reference(hamiltonian, cheb_low, cheb_high, pattern, atoms):
    flat_pattern = pattern.reshape(PIECES, GROUPS, 2, CAP)
    tile_rows = flat_pattern[:, :, 0, :]
    tile_cols = flat_pattern[:, :, 1, :]
    is_live = tile_rows >= 0
    piece_ids = jnp.arange(PIECES, dtype=jnp.int32)[:, None, None]
    group_ids = jnp.arange(GROUPS, dtype=jnp.int32)[None, :, None]
    slot_total = PIECES * GROUPS * CAP
    flat_ids = jnp.arange(slot_total, dtype=jnp.int32).reshape(PIECES, GROUPS, CAP)
    global_row = jnp.where(is_live, piece_ids * RB + tile_rows, NB).astype(jnp.int32)
    global_col = jnp.where(is_live, block_column(group_ids, tile_cols), NB).astype(jnp.int32)
    slot_table = jnp.full((NB, NB), slot_total, jnp.int32).at[global_row, global_col].set(flat_ids, mode="drop")
    row_ranks = rank_in_row(tile_rows)
    safe_rows = jnp.where(is_live, tile_rows, RB).astype(jnp.int32)
    right_table = jnp.full((PIECES, GROUPS, RB, SK), slot_total, jnp.int32)
    right_table = right_table.at[piece_ids, group_ids, safe_rows, row_ranks].set(flat_ids, mode="drop")
    low_flat = cheb_low.reshape(slot_total, TILE, TILE)
    col_flat = jnp.minimum(global_col.reshape(slot_total), NB - 1)

    def layer_partial(left_tiles, layer_id):
        def add_piece(piece_index, accumulator):
            left_here = lax.dynamic_index_in_dim(left_tiles, piece_index, 0, keepdims=False)
            rows_here = lax.dynamic_index_in_dim(tile_rows, piece_index, 0, keepdims=False)
            cols_here = lax.dynamic_index_in_dim(global_col, piece_index, 0, keepdims=False)
            table_here = lax.dynamic_index_in_dim(right_table, piece_index, 0, keepdims=False)
            live_here = rows_here >= 0
            clipped_rows = jnp.clip(rows_here, 0, RB - 1)
            clipped_cols = jnp.minimum(cols_here, NB - 1)
            left_wide = left_here.astype(jnp.float32)
            for other_group in range(GROUPS):
                for column in range(SK):
                    picked = table_here[other_group][clipped_rows, column]
                    usable = live_here & (picked < slot_total)
                    picked = jnp.minimum(picked, slot_total - 1)
                    target = jnp.where(usable, slot_table[clipped_cols, col_flat[picked]], slot_total)
                    right_tiles = low_flat[picked].astype(jnp.float32)
                    product = jnp.einsum("gcpx,gcpy->gcxy", left_wide, right_tiles, precision=lax.Precision.HIGHEST)
                    accumulator = accumulator.at[target.reshape(-1)].add(product.reshape(-1, TILE, TILE), mode="drop")
            return accumulator

        start = layer_id * ROWGROUPS
        return lax.fori_loop(start, start + ROWGROUPS, add_piece, jnp.zeros((slot_total, TILE, TILE), jnp.float32))

    def doubled(left_tiles):
        summed = jnp.zeros((slot_total, TILE, TILE), jnp.float32)
        for layer_id in range(LAYERS):
            partial_value = layer_partial(left_tiles, layer_id)
            rounded = lax.optimization_barrier(partial_value.astype(jnp.bfloat16))
            summed = summed + rounded.astype(jnp.float32)
        return summed.reshape(PIECES, GROUPS, CAP, TILE, TILE)

    sum_even = doubled(cheb_low)
    sum_odd = doubled(cheb_high)
    across = jnp.arange(TILE, dtype=jnp.int32)
    functions = FUNCS * atoms[jnp.minimum(global_row, NB - 1)]
    on_diagonal = is_live & (global_row == global_col)
    identity = (across[:, None] == across[None, :]) & (across[None, :] < functions[..., None, None])
    identity = jnp.where(on_diagonal[..., None, None] & identity, 1.0, 0.0).astype(jnp.float32)
    live_tiles = is_live[..., None, None]
    result_even = jnp.where(live_tiles, 2.0 * sum_even - identity, 0.0).astype(jnp.bfloat16)
    result_odd = jnp.where(live_tiles, 2.0 * sum_odd - hamiltonian.astype(jnp.float32), 0.0).astype(jnp.bfloat16)
    return result_even, result_odd
```

```python
import functools

import jax
import jax.numpy as jnp
from jax import lax
from jax.experimental import pallas as pl
from jax.experimental.pallas import tpu as pltpu
from jax.sharding import PartitionSpec as P

FUNCS = 8
SK = 1
TILE = 128
CAP = 23
RB = 96
LANES = 32
SPAN = 4
HALF = 12
LIST = 9
EXTRA = 2
BLOB = 2 * TILE + 16
BF = jnp.bfloat16
F32 = jnp.float32
I32 = jnp.int32
VM = pl.BlockSpec(memory_space=pltpu.VMEM)
SM = pl.BlockSpec(memory_space=pltpu.SMEM)
LIMIT = 56 * 1024 * 1024


def to_column(row, n):
    eye = lax.broadcasted_iota(I32, (n, n), 0) == lax.broadcasted_iota(I32, (n, n), 1)
    return jnp.sum(jnp.where(eye, row, 0.0), axis=1, keepdims=True)


def one(cond):
    return jnp.where(cond, 1.0, 0.0)


def piece_row(patterns, index, layer):
    both = patterns[pl.ds(index, 1), :]
    here = jnp.where(layer == 0, both[:, : 2 * LANES], both[:, 2 * LANES :])
    return here[:, :LANES], here[:, LANES:]


def positions(needed):
    rows = lax.broadcasted_iota(I32, (LANES, LANES), 0)
    lanes = lax.broadcasted_iota(I32, (LANES, LANES), 1)
    as_row = jnp.sum(jnp.where(rows == lanes, needed, 0.0), axis=0, keepdims=True)
    return jnp.sum(jnp.where(lanes < rows, as_row, 0.0), axis=1, keepdims=True)


def meta_block(fields):
    lanes = lax.broadcasted_iota(I32, (16, TILE), 1)
    block = jnp.zeros((16, TILE), F32)
    for i, value in enumerate(fields):
        block = jnp.where(lanes == i, value.astype(F32), block)
    return block.astype(BF)


BITS = (0, 1, 3, 5, 12, 13, 18, 20)
WIDE = (1, 2, 2, 7, 1, 5, 2, 1)


def read_meta(block):
    lanes = lax.broadcasted_iota(I32, (16, TILE), 1)
    weights = jnp.zeros((16, TILE), F32)
    for i, bit in enumerate(BITS):
        weights = jnp.where(lanes == i, float(1 << bit), weights)
    code = jnp.max(jnp.sum(block.astype(F32) * weights, axis=1, keepdims=True)).astype(I32)
    return [(code >> bit) & ((1 << wide) - 1) for bit, wide in zip(BITS, WIDE)]


def plan_kernel(where, own, patterns, low, high, table, extra):
    q, r, z, y = where[0], where[1], where[2], where[3]
    g = z * SPAN + y
    me = r * 16 + g
    own_k, own_j = piece_row(patterns, me, q)
    k_col, j_col = to_column(own_k, LANES), to_column(own_j, LANES)
    lanes = lax.broadcasted_iota(I32, (LANES, LANES), 1)
    slot_col = lax.broadcasted_iota(I32, (LANES, 1), 0).astype(F32)

    def center(s):
        ck, cj = piece_row(patterns, r * 20 + s, q)
        ck = jnp.where((ck >= 0) & (ck == cj), ck, -2.0)
        return to_column(ck, LANES)

    def needed_by(center_col, line_y):
        lk, lj = piece_row(patterns, r * 16 + z * SPAN + line_y, q)
        lk = jnp.where(lk == lj, -1.0, lk)
        return jnp.max(one(center_col == lk), axis=1, keepdims=True)

    table[...] = jnp.zeros_like(table)
    overflow = jnp.zeros((1, 1), F32)
    mine = center(y)
    for d in range(1, SPAN):
        needed = needed_by(mine, (y + d) % SPAN)
        pos = positions(needed)
        chosen = (needed > 0) & (pos.astype(I32) == lanes)
        entries = jnp.sum(jnp.where(chosen, slot_col, 0.0), axis=0, keepdims=True)
        table[d - 1 : d, :LANES] = entries.astype(I32)
        total = jnp.sum(needed, axis=0, keepdims=True)
        overflow = jnp.maximum(overflow, one(total > LIST))
    code = jnp.zeros((1, LANES), F32)
    own_off = jnp.where(own_k == own_j, -1.0, own_k)
    for d in range(SPAN):
        there = center((y + SPAN - d) % SPAN)
        needed = needed_by(there, y)
        if d:
            entry = 1.0 + LANES * d + positions(needed)
        else:
            entry = 1.0 + slot_col
        code = code + jnp.sum(jnp.where(there == own_off, entry, 0.0), axis=0, keepdims=True)
    table[3:4, :LANES] = code.astype(I32)

    outs = []
    for layer in range(2):
        ok, oj = piece_row(patterns, z * 16 + g, layer)
        outs.append(to_column(jnp.where(ok == oj, ok, -2.0), LANES))
    for i, step in enumerate((0, 1, 3, 2)):
        _, sj = piece_row(patterns, ((z + step) % SPAN) * 16 + g, q)
        target = jnp.zeros((1, LANES), F32)
        for layer in range(2):
            hit = (outs[layer] == sj) & (sj >= 0)
            target = target + jnp.sum(
                jnp.where(hit, 1.0 + LANES * layer + slot_col, 0.0), axis=0, keepdims=True
            )
        target = jnp.where(r == z, target, 0.0)
        table[4 + i : 5 + i, :LANES] = target.astype(I32)

    wide = lax.broadcasted_iota(I32, (LANES, 2 * LANES), 1)
    deep = lax.broadcasted_iota(I32, (LANES, 2 * LANES), 0)
    first = jnp.zeros((LANES, 2 * LANES), F32)
    second = jnp.zeros((LANES, 2 * LANES), F32)
    lefts = jnp.zeros((LANES, 2 * LANES), F32)
    rights = jnp.zeros((LANES, 2 * LANES), F32)

    def out_rows(row):
        ks = jnp.concatenate([row[:, :LANES], row[:, 2 * LANES : 3 * LANES]], axis=1)
        js = jnp.concatenate([row[:, LANES : 2 * LANES], row[:, 3 * LANES :]], axis=1)
        return ks, js

    for other in range(16):
        uk, uj = piece_row(patterns, r * 16 + other, q)
        partner = jnp.sum(jnp.where((k_col == uk) & (uk >= 0), uj + 1.0, 0.0), axis=1, keepdims=True) - 1.0
        vk, vj = out_rows(patterns[pl.ds(z * 16 + other, 1), :])
        hit = (partner == vj) & (vk == j_col) & (vk >= 0)
        hit = hit & (partner != j_col) & (j_col != k_col)
        lefts = lefts + one(hit)
        entry = jnp.where(hit, (1 + deep + LANES * wide + 2048 * other).astype(F32), 0.0)
        second = jnp.maximum(second, jnp.minimum(first, entry))
        first = jnp.maximum(first, entry)
        wk, wj = out_rows(patterns[pl.ds((other // SPAN) * 16 + g, 1), :])
        hit = (partner == wk) & (wj == j_col) & (wj >= 0)
        hit = hit & (partner != j_col) & (partner != k_col)
        rights = rights + one(hit)
    many = jnp.maximum(one(jnp.sum(lefts) > EXTRA), one(jnp.sum(rights) > EXTRA))
    flag = jnp.maximum(jnp.max(overflow), many)
    top = jnp.max(first)
    next_top = jnp.maximum(jnp.max(jnp.where(first == top, 0.0, first)), jnp.max(second))
    for i, best in enumerate((top, next_top)):
        entry = best.astype(I32)
        valid = jnp.minimum(entry, 1)
        entry = jnp.maximum(entry - 1, 0)
        left = entry % LANES
        out = (entry // LANES) % (2 * LANES)
        to = entry // 2048
        left = jnp.minimum(left, CAP - 1)
        row = jnp.maximum(own[2 * q, left], 0)
        extra[i, :TILE, :] = low[left]
        extra[i, TILE : 2 * TILE, :] = high[left]
        extra[i, 2 * TILE :, :] = meta_block(
            (valid, to // SPAN, to % SPAN, row, out // LANES, out % LANES, z, flag)
        )


def pack_kernel(where, table, own, p1, p2, p3, p4, b1, b2, b3):
    kind = (where[1] - where[2] + SPAN) % SPAN
    for d, buffer in enumerate((b1, b2, b3)):

        def step(j, _, d=d, buffer=buffer):
            m = jnp.minimum(table[d, j], CAP - 1)
            copy_left(kind, m, own, p1, p2, p3, p4, buffer, j)
            return 0

        lax.fori_loop(0, LIST, step, 0)


def copy_left(kind, m, own, p1, p2, p3, p4, buffer, j):
    @pl.when(kind == 0)
    def _():
        buffer[j] = own[m]

    @pl.when(kind == 3)
    def _():
        buffer[j] = p1[m]

    @pl.when(kind == 1)
    def _():
        buffer[j] = p2[m]

    @pl.when((kind == 2) & (m < HALF))
    def _():
        buffer[j] = p3[jnp.minimum(m, HALF - 1)]

    @pl.when((kind == 2) & (m >= HALF))
    def _():
        buffer[j] = p4[jnp.maximum(m - HALF, 0)]


def forward_kernel(where, e0, e1, e2, e3, b0, b1, b2, b3):
    z, y = where[2], where[3]
    metas = [read_meta(e[i, 2 * TILE :, :]) for e in (e0, e1, e2, e3) for i in range(EXTRA)]
    flag = functools.reduce(jnp.maximum, [m[7] for m in metas])
    zero = jnp.int32(0)
    for d, buffer in enumerate((b0, b1, b2, b3)):
        for i in range(EXTRA):
            buffer[i] = jnp.zeros((BLOB, TILE), BF)
            buffer[i, 2 * TILE :, :] = meta_block((zero,) * 7 + (flag,))
        count = jnp.int32(0)
        for n, e in enumerate((e0, e1, e2, e3)):
            for i in range(EXTRA):
                m = metas[n * EXTRA + i]
                take = (m[0] > 0) & (m[1] == z) & (m[2] == (y + d) % SPAN)

                @pl.when(take & (count < EXTRA))
                def _(buffer=buffer, e=e, i=i, m=m, count=count):
                    buffer[count, : 2 * TILE, :] = e[i, : 2 * TILE, :]
                    buffer[count, 2 * TILE :, :] = meta_block((*m[:7], flag))

                count = count + take.astype(I32)


def contract(left, right):
    return lax.dot_general(left, right, (((0,), (0,)), ((), ())), preferred_element_type=F32)


def extra_kernel(where, own, low, e0, e1, e2, e3, result):
    q = where[0]
    metas = [read_meta(e[i, 2 * TILE :, :]) for e in (e0, e1, e2, e3) for i in range(EXTRA)]
    flag = functools.reduce(jnp.maximum, [m[7] for m in metas])
    zero = jnp.int32(0)
    for i in range(EXTRA):
        result[i] = jnp.zeros((BLOB, TILE), BF)
        result[i, 2 * TILE :, :] = meta_block((zero,) * 7 + (flag,))
    count = jnp.int32(0)
    for n, e in enumerate((e0, e1, e2, e3)):
        for i in range(EXTRA):
            m = metas[n * EXTRA + i]
            take = m[0] > 0

            @pl.when(take & (count < EXTRA))
            def _(e=e, i=i, m=m, count=count):
                def find(t, at):
                    return jnp.where(own[2 * q, t] == m[3], t, at)

                right = low[lax.fori_loop(0, CAP, find, jnp.int32(0))]
                for half in range(2):
                    rows = slice(half * TILE, (half + 1) * TILE)
                    result[count, rows, :] = contract(e[i, rows, :], right).astype(BF)
                result[count, 2 * TILE :, :] = meta_block((*m[:7], flag))

            count = count + take.astype(I32)


def self_kernel(where, table, own, p1, p2, p3, p4, rown, r1, r2, r3, r4, mine, theirs, sums):
    q = where[0]

    @pl.when(where[1] == where[2])
    def _():
        sums[...] = jnp.zeros_like(sums)

        def step(i, left, right, offset):
            def body(t, _):
                target = table[i, t + offset]

                @pl.when(target > 0)
                def _():
                    sums[target - 1] += contract(left[t], right[t])

                return 0

            lax.fori_loop(0, left.shape[0], body, 0)

        step(4, own, rown, 0)
        step(5, p1, r1, 0)
        step(6, p2, r2, 0)
        step(7, p3, r3, 0)
        step(7, p4, r4, HALF)
        for t in range(CAP):
            mine[t] = sums[q * LANES + t]
            theirs[t] = sums[(1 - q) * LANES + t].astype(BF)


def final_kernel(odd, where, own, atoms, table, low, left, p1, p2, p3, p4, b1, b2, b3,
                 mine, theirs, here, there, ham, out, total, tile):
    q, r, z, y = where[0], where[1], where[2], where[3]
    kind = (r - z + SPAN) % SPAN

    @pl.when(kind == 0)
    def _():
        def body(t, _):
            total[t] = mine[t] + theirs[t].astype(F32)
            return 0

        lax.fori_loop(0, CAP, body, 0)

    @pl.when(kind != 0)
    def _():
        total[...] = jnp.zeros_like(total)

    def product(t, _):
        code = table[3, t] - 1

        @pl.when(code >= 0)
        def _():
            d, m = code // LANES, jnp.minimum(code % LANES, CAP - 1)

            @pl.when(d == 0)
            def _():
                copy_left(kind, m, left, p1, p2, p3, p4, tile, 0)

            for i, buffer in enumerate((b1, b2, b3)):

                @pl.when(d == i + 1)
                def _(buffer=buffer):
                    tile[0] = buffer[jnp.minimum(m, LIST - 1)]

            total[t] += contract(tile[0], low[t])

        return 0

    lax.fori_loop(0, CAP, product, 0)
    for e in (here, there):
        for i in range(SPAN * EXTRA):
            m = read_meta(e[i, 2 * TILE :, :])

            @pl.when((m[0] > 0) & (m[4] == q) & (m[6] == r))
            def _(e=e, i=i, m=m):
                rows = slice(odd * TILE, (odd + 1) * TILE)
                slot = jnp.minimum(m[5], CAP - 1)
                total[slot] += e[i, rows, :].astype(F32)

    rows = lax.broadcasted_iota(I32, (TILE, TILE), 0)
    lanes = lax.broadcasted_iota(I32, (TILE, TILE), 1)
    diagonal = rows == lanes

    def finish(t, _):
        a, b = own[2 * q, t], own[2 * q + 1, t]

        @pl.when(a >= 0)
        def _():
            if odd:
                taken = ham[t].astype(F32)
            else:
                col = (b // 24 * SPAN + z) * RB + y * 24 + b % 24
                on = (q * SPAN + r) * RB + a == col
                functions = jnp.where(on, FUNCS * atoms[a], 0)
                taken = one(diagonal & (lanes < functions))
            out[t] = (2.0 * total[t] - taken).astype(BF)

        @pl.when(a < 0)
        def _():
            out[t] = jnp.zeros((TILE, TILE), BF)

        return 0

    lax.fori_loop(0, CAP, finish, 0)


def flag_kernel(here, there, flag):
    worst = jnp.int32(0)
    for e in (here, there):
        for i in range(0, SPAN * EXTRA, EXTRA):
            worst = jnp.maximum(worst, read_meta(e[i, 2 * TILE :, :])[7])
    flag[0, 0] = worst


def call(kernel, outs, ins, out_specs=None, scratch=(), name=None):
    return pl.pallas_call(
        kernel,
        out_shape=outs,
        in_specs=ins,
        out_specs=out_specs if out_specs is not None else jax.tree.map(lambda _: VM, outs),
        scratch_shapes=list(scratch),
        compiler_params=pltpu.CompilerParams(vmem_limit_bytes=LIMIT),
        name=name,
    )


def plane(move):
    pairs = []
    for x in range(SPAN):
        for z in range(SPAN):
            to = move((x - z) % SPAN, x, z)
            if to is not None:
                for y in range(SPAN):
                    pairs.append(((x * SPAN + z) * SPAN + y, ((to[0] % SPAN) * SPAN + to[1] % SPAN) * SPAN + y))
    return pairs


STEP1 = plane(lambda k, x, z: {0: (x, z + 1), 1: (z, z), 2: (z + 1, z)}.get(k))
STEP2 = plane(lambda k, x, z: {0: (x, z - 1), 3: (z, z), 2: (z - 1, z)}.get(k))
STEP3 = plane(lambda k, x, z: {3: (x, z + 1), 1: (z, z)}.get(k))
STEP4 = plane(lambda k, x, z: {1: (x, z - 1), 3: (z, z)}.get(k))


def along_z(d):
    return [(z * SPAN + y, (z + d) % SPAN * SPAN + y) for z in range(SPAN) for y in range(SPAN)]


def along_y(d):
    return [(z * SPAN + y, z * SPAN + (y + d) % SPAN) for z in range(SPAN) for y in range(SPAN)]


def along_x(d):
    return [(x, (x + d) % SPAN) for x in range(SPAN)]


def spread_tiles(tiles):
    axes = ("row", "col")
    p1 = lax.ppermute(tiles, axes, STEP1)
    p2 = lax.ppermute(tiles, axes, STEP2)
    p3 = lax.ppermute(p1[:HALF], axes, STEP3)
    p4 = lax.ppermute(p2[HALF:], axes, STEP4)
    return p1, p2, p3, p4


def sparse(hamiltonian, cheb_low, cheb_high, pattern, atoms):
    shape = jax.ShapeDtypeStruct
    tiles = (CAP, TILE, TILE)
    low = cheb_low.reshape(tiles)
    high = cheb_high.reshape(tiles)
    ham = hamiltonian.reshape(tiles)
    layer, x, col = (lax.axis_index(a) for a in ("layer", "row", "col"))
    where = jnp.stack([layer, x, col // SPAN, col % SPAN]).astype(I32)
    own = pattern.reshape(4, CAP)
    a, b = pattern[:, 0, 0, 0, :], pattern[:, 0, 0, 1, :]
    k = (jnp.arange(2, dtype=I32)[:, None] * SPAN + x) * RB + a
    j = (b // 24 * SPAN + col // SPAN) * RB + col % SPAN * 24 + b % 24
    live = (a >= 0)[:, None, :]
    named = jnp.where(live, jnp.stack([k, j], axis=1), -1).astype(F32)
    named = jnp.pad(named, ((0, 0), (0, 0), (0, LANES - CAP)), constant_values=-1.0)
    named = jnp.broadcast_to(named.reshape(1, 4 * LANES), (64, 4 * LANES))
    lows = spread_tiles(low)
    patterns = lax.all_to_all(named, ("row", "col"), 0, 0, tiled=True)
    highs = spread_tiles(high)

    blob = shape((EXTRA, BLOB, TILE), BF)
    table, extra = call(
        plan_kernel, (shape((8, TILE), I32), blob), [SM, SM, VM, VM, VM], name="plan"
    )(where, own, patterns, low, high)
    arrived = [lax.ppermute(extra, "col", along_z(d)) for d in (1, 2, 3)]
    forward = call(forward_kernel, (blob,) * 4, [SM] + [VM] * 4, name="forward")(where, extra, *arrived)
    arrived = [lax.ppermute(forward[d], "col", along_y(d)) for d in (1, 2, 3)]
    result = call(extra_kernel, blob, [SM, SM] + [VM] * 5, name="extra")(
        where, own, low, forward[0], *arrived
    )
    here = jnp.concatenate([result] + [lax.ppermute(result, "row", along_x(d)) for d in (1, 2, 3)])
    there = lax.ppermute(here, "layer", [(0, 1), (1, 0)])
    flag = call(flag_kernel, shape((1, 1), I32), [VM, VM], out_specs=SM, name="flag")(here, there)

    lists = shape((LIST, TILE, TILE), BF)
    results = []
    for odd, (left, spread) in enumerate(((low, lows), (high, highs))):
        packed = call(pack_kernel, (lists,) * 3, [SM, SM] + [VM] * 5, name="pack")(
            where, table, left, *spread
        )
        lines = [lax.ppermute(packed[d - 1], "col", along_y(d)) for d in (1, 2, 3)]
        mine, theirs = call(
            self_kernel,
            (shape(tiles, F32), shape(tiles, BF)),
            [SM, SM] + [VM] * 10,
            scratch=[pltpu.VMEM((2 * LANES, TILE, TILE), F32)],
            name="squares",
        )(where, table, left, *spread, low, *lows)
        theirs = lax.ppermute(theirs, "layer", [(0, 1), (1, 0)])
        results.append(
            call(
                functools.partial(final_kernel, odd),
                shape(tiles, BF),
                [SM] * 4 + [VM] * 14,
                scratch=[pltpu.VMEM(tiles, F32), pltpu.VMEM((1, TILE, TILE), BF)],
                name="finish",
            )(where, own, atoms, table, low, left, *spread, *lines, mine, theirs, here, there, ham)
        )
    return flag, [out[None, None] for out in results]


def spread_2(array, axis, root):
    mine = lax.axis_index(axis) == root
    return lax.psum(jnp.where(mine, array, jnp.zeros_like(array)), axis)


def rank_in_row(row_ids):
    earlier = jnp.arange(row_ids.shape[-1], dtype=jnp.int32)
    matches = (row_ids[..., :, None] == row_ids[..., None, :]) & (
        earlier[None, :] < earlier[:, None]
    )
    return jnp.sum(matches.astype(jnp.int32), axis=-1)


def panels(hamiltonian, cheb_low, cheb_high, pattern, atoms):
    block_rows = atoms.shape[0]
    capacity = pattern.shape[-1]
    tile_size = cheb_low.shape[-1]
    grid_rows = lax.axis_size("row")
    grid_cols = lax.axis_size("col")
    layer_count = lax.axis_size("layer")
    spread = grid_cols // grid_rows
    sub_rows = block_rows // spread
    col_width = layer_count * sub_rows
    row_index = lax.axis_index("row")
    col_index = lax.axis_index("col")
    layer_index = lax.axis_index("layer")
    own_pattern = lax.dynamic_index_in_dim(pattern[:, 0, 0], layer_index, 0, keepdims=True)[:, None]
    low_panel, high_panel, index_panel = (
        lax.all_gather(cheb_low, "row", axis=0, tiled=True),
        lax.all_gather(cheb_high, "row", axis=0, tiled=True),
        lax.all_gather(own_pattern, "row", axis=0, tiled=True),
    )
    arrivals = []
    for offset in range(spread):
        arrivals.append(
            (
                spread_2(low_panel, "col", row_index * spread + offset),
                spread_2(high_panel, "col", row_index * spread + offset),
                spread_2(index_panel, "col", row_index * spread + offset),
            )
        )
    high_blocks = [arrival[1][:, 0] for arrival in arrivals]
    low_blocks = [arrival[0][:, 0] for arrival in arrivals]
    index_left = jnp.concatenate([arrival[-1] for arrival in arrivals], axis=1)
    right_rows = index_panel[:, 0, 0, :]
    right_cols = index_panel[:, 0, 1, :]
    right_live = right_rows >= 0
    right_rank = rank_in_row(right_rows)
    right_count = grid_rows * capacity
    piece_ids = jnp.arange(grid_rows, dtype=jnp.int32)[:, None]
    tile_ids = piece_ids * capacity + jnp.arange(capacity, dtype=jnp.int32)[None, :]
    safe_rows = jnp.where(right_live, right_rows, block_rows)
    right_table = jnp.full((grid_rows, block_rows, SK), right_count, jnp.int32)
    right_table = right_table.at[piece_ids, safe_rows, right_rank].set(tile_ids, mode="drop")
    right_table = right_table.reshape(grid_rows * block_rows, SK)
    right_flat = low_panel.reshape(right_count, tile_size, tile_size)
    right_cols_flat = right_cols.reshape(right_count)
    out_rows = pattern[:, 0, 0, 0, :]
    out_cols = pattern[:, 0, 0, 1, :]
    layer_ids = jnp.arange(layer_count, dtype=jnp.int32)[:, None]
    out_local = jnp.where(
        out_rows >= 0, layer_ids * block_rows + out_rows, layer_count * block_rows
    )
    slot_total = layer_count * capacity
    slot_ids = layer_ids * capacity + jnp.arange(capacity, dtype=jnp.int32)[None, :]
    slot_table = jnp.full((layer_count * block_rows, col_width), slot_total, jnp.int32)
    slot_table = slot_table.at[out_local, out_cols].set(slot_ids, mode="drop")
    left_rows = index_left[:, :, 0, :]
    left_cols = index_left[:, :, 1, :]
    left_live = left_rows >= 0
    spread_ids = jnp.arange(spread, dtype=jnp.int32)[None, :, None]
    left_piece = jnp.arange(grid_rows, dtype=jnp.int32)[:, None, None]
    inner_rows = left_piece * block_rows + jnp.clip(left_rows, 0, block_rows - 1)
    target_rows = left_cols // sub_rows * block_rows + spread_ids * sub_rows + left_cols % sub_rows
    target_rows = jnp.where(left_live, target_rows, 0)
    even_sum = jnp.zeros((slot_total, tile_size, tile_size), jnp.float32)
    odd_sum = jnp.zeros((slot_total, tile_size, tile_size), jnp.float32)
    for offset in range(spread):
        block_inner = inner_rows[:, offset].reshape(-1)
        block_target = target_rows[:, offset].reshape(-1)
        block_valid = left_live[:, offset].reshape(-1)
        low_tiles = low_blocks[offset].reshape(-1, tile_size, tile_size)
        high_tiles = high_blocks[offset].reshape(-1, tile_size, tile_size)
        picked = right_table[block_inner, 0]
        usable = block_valid & (picked < right_count)
        picked = jnp.minimum(picked, right_count - 1)
        target = jnp.where(
            usable, slot_table[block_target, jnp.maximum(right_cols_flat[picked], 0)], slot_total
        )
        right_tiles = right_flat[picked]
        even_sum = even_sum.at[target].add(
            jnp.einsum("npx,npy->nxy", low_tiles, right_tiles, preferred_element_type=jnp.float32),
            mode="drop",
        )
        odd_sum = odd_sum.at[target].add(
            jnp.einsum("npx,npy->nxy", high_tiles, right_tiles, preferred_element_type=jnp.float32),
            mode="drop",
        )
    even_total, odd_total = (
        lax.psum_scatter(
            even_sum.astype(jnp.bfloat16), "layer", scatter_dimension=0, tiled=True
        ).astype(jnp.float32),
        lax.psum_scatter(
            odd_sum.astype(jnp.bfloat16), "layer", scatter_dimension=0, tiled=True
        ).astype(jnp.float32),
    )
    own_rows = own_pattern[0, 0, 0, :]
    own_cols = own_pattern[0, 0, 1, :]
    own_live = own_rows >= 0
    global_row = (layer_index * grid_rows + row_index) * block_rows + own_rows
    global_col = (
        (own_cols // sub_rows * grid_rows + col_index // spread) * block_rows
        + col_index % spread * sub_rows
        + own_cols % sub_rows
    )
    on_diagonal = own_live & (global_row == global_col)
    functions = FUNCS * atoms[jnp.clip(own_rows, 0, block_rows - 1)]
    across = jnp.arange(tile_size, dtype=jnp.int32)
    identity = (across[:, None] == across[None, :]) & (
        across[None, None, :] < functions[:, None, None]
    )
    identity = jnp.where(on_diagonal[:, None, None] & identity, 1.0, 0.0).astype(jnp.float32)
    live_tiles = own_live[:, None, None]
    result_even = jnp.where(live_tiles, 2.0 * even_total - identity, 0.0).astype(jnp.bfloat16)
    result_odd = jnp.where(
        live_tiles, 2.0 * odd_total - hamiltonian[0, 0].astype(jnp.float32), 0.0
    ).astype(jnp.bfloat16)
    return (result_even[None, None], result_odd[None, None])


def shards(hamiltonian, cheb_low, cheb_high, pattern, atoms):
    flag, (even, odd) = sparse(hamiltonian, cheb_low, cheb_high, pattern, atoms)
    return lax.cond(
        flag[0, 0] > 0,
        lambda: panels(hamiltonian, cheb_low, cheb_high, pattern, atoms),
        lambda: (even, odd),
    )


def solution(mesh):
    return jax.shard_map(
        shards,
        mesh=mesh,
        in_specs=(
            P(("layer", "row"), "col", None, None, None),
            P(("layer", "row"), "col", None, None, None),
            P(("layer", "row"), "col", None, None, None),
            P(None, "row", "col", None, None),
            P(("layer", "row")),
        ),
        out_specs=(
            P(("layer", "row"), "col", None, None, None),
            P(("layer", "row"), "col", None, None, None),
        ),
        check_vma=False,
    )
```

```python
import functools

import jax
import jax.numpy as jnp
from jax import lax
from jax.experimental import pallas as pl
from jax.experimental.pallas import tpu as pltpu
from jax.sharding import PartitionSpec as P

FUNCS = 8
SK = 1
TILE = 128
CAP = 23
RB = 96
LANES = 32
SPAN = 4
HALF = 12
LIST = 10
EXTRA = 2
BLOB = 2 * TILE + 16
BF = jnp.bfloat16
F32 = jnp.float32
I32 = jnp.int32
VM = pl.BlockSpec(memory_space=pltpu.VMEM)
SM = pl.BlockSpec(memory_space=pltpu.SMEM)
HB = pl.BlockSpec(memory_space=pl.ANY)
LIMIT = 56 * 1024 * 1024


def to_column(row, n):
    eye = lax.broadcasted_iota(I32, (n, n), 0) == lax.broadcasted_iota(I32, (n, n), 1)
    return jnp.sum(jnp.where(eye, row, 0.0), axis=1, keepdims=True)


def one(cond):
    return jnp.where(cond, 1.0, 0.0)


def piece_row(patterns, index, layer):
    both = patterns[pl.ds(index, 1), :]
    here = jnp.where(layer == 0, both[:, : 2 * LANES], both[:, 2 * LANES :])
    return here[:, :LANES], here[:, LANES:]


def positions(needed):
    rows = lax.broadcasted_iota(I32, (LANES, LANES), 0)
    lanes = lax.broadcasted_iota(I32, (LANES, LANES), 1)
    as_row = jnp.sum(jnp.where(rows == lanes, needed, 0.0), axis=0, keepdims=True)
    return jnp.sum(jnp.where(lanes < rows, as_row, 0.0), axis=1, keepdims=True)


def meta_block(fields):
    lanes = lax.broadcasted_iota(I32, (16, TILE), 1)
    block = jnp.zeros((16, TILE), F32)
    for i, value in enumerate(fields):
        block = jnp.where(lanes == i, value.astype(F32), block)
    return block.astype(BF)


BITS = (0, 1, 3, 5, 12, 13, 18, 20)
WIDE = (1, 2, 2, 7, 1, 5, 2, 1)


def read_meta(block):
    lanes = lax.broadcasted_iota(I32, (16, TILE), 1)
    weights = jnp.zeros((16, TILE), F32)
    for i, bit in enumerate(BITS):
        weights = jnp.where(lanes == i, float(1 << bit), weights)
    code = jnp.max(jnp.sum(block.astype(F32) * weights, axis=1, keepdims=True)).astype(I32)
    return [(code >> bit) & ((1 << wide) - 1) for bit, wide in zip(BITS, WIDE)]


def plan_kernel(where, own, g0, g1, g2, g3, low, high, table, extra, patterns, sems):
    q, r, z, y = where[0], where[1], where[2], where[3]
    for d, rows in enumerate((g0, g1, g2, g3)):
        patterns[16 * d : 16 * (d + 1), :] = rows[...]

    def row(to_x, to_z, to_y):
        dx, dz, dy = ((a - b + SPAN) % SPAN for a, b in ((r, to_x), (z, to_z), (y, to_y)))
        return dy * 16 + dz * SPAN + dx

    own_k, own_j = piece_row(patterns, 0, q)
    k_col, j_col = to_column(own_k, LANES), to_column(own_j, LANES)
    lanes = lax.broadcasted_iota(I32, (LANES, LANES), 1)
    slot_col = lax.broadcasted_iota(I32, (LANES, 1), 0).astype(F32)

    def center(s):
        ck, cj = piece_row(patterns, row(r, r, s), q)
        ck = jnp.where((ck >= 0) & (ck == cj), ck, -2.0)
        return to_column(ck, LANES)

    def needed_by(center_col, line_y):
        lk, lj = piece_row(patterns, row(r, z, line_y), q)
        lk = jnp.where(lk == lj, -1.0, lk)
        return jnp.max(one(center_col == lk), axis=1, keepdims=True)

    table[...] = jnp.zeros_like(table)
    overflow = jnp.zeros((1, 1), F32)
    mine = center(y)
    for d in range(1, SPAN):
        needed = needed_by(mine, (y + d) % SPAN)
        pos = positions(needed)
        chosen = (needed > 0) & (pos.astype(I32) == lanes)
        entries = jnp.sum(jnp.where(chosen, slot_col, 0.0), axis=0, keepdims=True)
        table[d - 1 : d, :LANES] = entries.astype(I32)
        total = jnp.sum(needed, axis=0, keepdims=True)
        overflow = jnp.maximum(overflow, one(total > LIST))
    code = jnp.zeros((1, LANES), F32)
    own_off = jnp.where(own_k == own_j, -1.0, own_k)
    for d in range(SPAN):
        there = center((y + SPAN - d) % SPAN)
        needed = needed_by(there, y)
        if d:
            entry = 1.0 + LANES * d + positions(needed)
        else:
            entry = 1.0 + slot_col
        code = code + jnp.sum(jnp.where(there == own_off, entry, 0.0), axis=0, keepdims=True)
    table[3:4, :LANES] = code.astype(I32)

    outs = []
    for layer in range(2):
        ok, oj = piece_row(patterns, row(z, z, y), layer)
        outs.append(to_column(jnp.where(ok == oj, ok, -2.0), LANES))
    for i, step in enumerate((0, 1, 3, 2)):
        _, sj = piece_row(patterns, row((z + step) % SPAN, z, y), q)
        target = jnp.zeros((1, LANES), F32)
        for layer in range(2):
            hit = (outs[layer] == sj) & (sj >= 0)
            target = target + jnp.sum(
                jnp.where(hit, 1.0 + LANES * layer + slot_col, 0.0), axis=0, keepdims=True
            )
        target = jnp.where(r == z, target, 0.0)
        table[4 + i : 5 + i, :LANES] = target.astype(I32)

    wide = lax.broadcasted_iota(I32, (LANES, 2 * LANES), 1)
    deep = lax.broadcasted_iota(I32, (LANES, 2 * LANES), 0)
    first = jnp.zeros((LANES, 2 * LANES), F32)
    second = jnp.zeros((LANES, 2 * LANES), F32)
    lefts = jnp.zeros((LANES, 2 * LANES), F32)
    rights = jnp.zeros((LANES, 2 * LANES), F32)

    def out_rows(row):
        ks = jnp.concatenate([row[:, :LANES], row[:, 2 * LANES : 3 * LANES]], axis=1)
        js = jnp.concatenate([row[:, LANES : 2 * LANES], row[:, 3 * LANES :]], axis=1)
        return ks, js

    for other in range(16):
        uk, uj = piece_row(patterns, row(r, other // SPAN, other % SPAN), q)
        partner = jnp.sum(jnp.where((k_col == uk) & (uk >= 0), uj + 1.0, 0.0), axis=1, keepdims=True) - 1.0
        vk, vj = out_rows(patterns[pl.ds(row(z, other // SPAN, other % SPAN), 1), :])
        hit = (partner == vj) & (vk == j_col) & (vk >= 0)
        hit = hit & (partner != j_col) & (j_col != k_col)
        lefts = lefts + one(hit)
        entry = jnp.where(hit, (1 + deep + LANES * wide + 2048 * other).astype(F32), 0.0)
        second = jnp.maximum(second, jnp.minimum(first, entry))
        first = jnp.maximum(first, entry)
        wk, wj = out_rows(patterns[pl.ds(row(other // SPAN, z, y), 1), :])
        hit = (partner == wk) & (wj == j_col) & (wj >= 0)
        hit = hit & (partner != j_col) & (partner != k_col)
        rights = rights + one(hit)
    many = jnp.maximum(one(jnp.sum(lefts) > EXTRA), one(jnp.sum(rights) > EXTRA))
    flag = jnp.maximum(jnp.max(overflow), many)
    top = jnp.max(first)
    next_top = jnp.maximum(jnp.max(jnp.where(first == top, 0.0, first)), jnp.max(second))
    for i, best in enumerate((top, next_top)):
        entry = best.astype(I32)
        valid = jnp.minimum(entry, 1)
        entry = jnp.maximum(entry - 1, 0)
        left = entry % LANES
        out = (entry // LANES) % (2 * LANES)
        dest = entry // 2048
        left = jnp.minimum(left, CAP - 1)
        at_row = jnp.maximum(own[2 * q, left], 0)
        for half, tiles in enumerate((low, high)):
            to = extra.at[i, pl.ds(half * TILE, TILE), :]
            pltpu.make_async_copy(tiles.at[left], to, sems.at[2 * i + half]).start()
        extra[i, 2 * TILE :, :] = meta_block(
            (valid, dest // SPAN, dest % SPAN, at_row, out // LANES, out % LANES, z, flag)
        )
    for i in range(EXTRA):
        for half, tiles in enumerate((low, high)):
            to = extra.at[i, pl.ds(half * TILE, TILE), :]
            pltpu.make_async_copy(tiles.at[0], to, sems.at[2 * i + half]).wait()


REST = CAP - HALF
LOW_PARTS = (((1, 0, 0, CAP),), ((2, 0, 0, CAP),), ((3, HALF, 0, HALF),), ((3, REST, HALF, REST),))
HIGH_PARTS = (
    ((1, 0, 0, HALF),),
    ((2, 0, HALF, REST),),
    ((1, 0, HALF, REST), (3, REST, 0, HALF)),
    ((2, 0, 0, HALF), (3, HALF, HALF, REST)),
)
FROM_CENTER = {1: 2, 2: 3, 3: 1}


def copy_left(kind, m, parts, own, spread, to, sem):
    @pl.when(kind == 0)
    def _():
        pltpu.make_async_copy(own.at[m], to, sem).start()

    for other, source in FROM_CENTER.items():
        for array, pieces in zip(spread, parts):
            for origin, row, slot, count in pieces:
                if origin == source:

                    @pl.when((kind == other) & (m >= slot) & (m < slot + count))
                    def _(array=array, row=row, slot=slot, count=count):
                        at = row + jnp.clip(m - slot, 0, count - 1)
                        pltpu.make_async_copy(array.at[at], to, sem).start()


def pack_kernel(parts, where, table, own, s1, s2, s3, s4, b1, b2, b3, sems):
    kind = (where[1] - where[2] + SPAN) % SPAN
    for d, buffer in enumerate((b1, b2, b3)):
        for j in range(LIST):
            m = jnp.minimum(table[d, j], CAP - 1)
            copy_left(kind, m, parts, own, (s1, s2, s3, s4), buffer.at[j], sems.at[d * LIST + j])
    for d, buffer in enumerate((b1, b2, b3)):
        for j in range(LIST):
            pltpu.make_async_copy(own.at[0], buffer.at[j], sems.at[d * LIST + j]).wait()


def forward_kernel(where, e0, e1, e2, e3, b0, b1, b2, b3):
    z, y = where[2], where[3]
    metas = [read_meta(e[i, 2 * TILE :, :]) for e in (e0, e1, e2, e3) for i in range(EXTRA)]
    flag = functools.reduce(jnp.maximum, [m[7] for m in metas])
    zero = jnp.int32(0)
    for d, buffer in enumerate((b0, b1, b2, b3)):
        for i in range(EXTRA):
            buffer[i] = jnp.zeros((BLOB, TILE), BF)
            buffer[i, 2 * TILE :, :] = meta_block((zero,) * 7 + (flag,))
        count = jnp.int32(0)
        for n, e in enumerate((e0, e1, e2, e3)):
            for i in range(EXTRA):
                m = metas[n * EXTRA + i]
                take = (m[0] > 0) & (m[1] == z) & (m[2] == (y + d) % SPAN)

                @pl.when(take & (count < EXTRA))
                def _(buffer=buffer, e=e, i=i, m=m, count=count):
                    buffer[count, : 2 * TILE, :] = e[i, : 2 * TILE, :]
                    buffer[count, 2 * TILE :, :] = meta_block((*m[:7], flag))

                count = count + take.astype(I32)


def contract(left, right):
    return lax.dot_general(left, right, (((0,), (0,)), ((), ())), preferred_element_type=F32)


def extra_kernel(where, own, low, e0, e1, e2, e3, result):
    q = where[0]
    metas = [read_meta(e[i, 2 * TILE :, :]) for e in (e0, e1, e2, e3) for i in range(EXTRA)]
    flag = functools.reduce(jnp.maximum, [m[7] for m in metas])
    zero = jnp.int32(0)
    for i in range(EXTRA):
        result[i] = jnp.zeros((BLOB, TILE), BF)
        result[i, 2 * TILE :, :] = meta_block((zero,) * 7 + (flag,))
    count = jnp.int32(0)
    for n, e in enumerate((e0, e1, e2, e3)):
        for i in range(EXTRA):
            m = metas[n * EXTRA + i]
            take = m[0] > 0

            @pl.when(take & (count < EXTRA))
            def _(e=e, i=i, m=m, count=count):
                def find(t, at):
                    return jnp.where(own[2 * q, t] == m[3], t, at)

                right = low[lax.fori_loop(0, CAP, find, jnp.int32(0))]
                for half in range(2):
                    rows = slice(half * TILE, (half + 1) * TILE)
                    result[count, rows, :] = contract(e[i, rows, :], right).astype(BF)
                result[count, 2 * TILE :, :] = meta_block((*m[:7], flag))

            count = count + take.astype(I32)


def square_kernel(where, left, low, product, send):
    center = where[1] == where[2]
    for t in range(CAP):
        product[t] = contract(left[t], low[t]).astype(BF)

    @pl.when(center)
    def _():
        send[...] = left[...]

    @pl.when(jnp.logical_not(center))
    def _():
        send[...] = product[...]


def collect_kernel(odd, parts, where, table, own, s1, s2, s3, s4, e0, e1, e2, e3,
                   mine, theirs, flag, sums, tiles, sems):
    q, r = where[0], where[1]
    center = r == where[2]
    sources = (own, s1, s2, s3, s4)

    def copies():
        return [
            pltpu.make_async_copy(array, tiles.at[i, pl.ds(0, array.shape[0])], sems.at[i])
            for i, array in enumerate(sources)
        ]

    @pl.when(center)
    def _():
        for copy in copies():
            copy.start()

    sums[...] = jnp.zeros_like(sums)
    metas = [read_meta(e[i, 2 * TILE :, :]) for e in (e0, e1, e2, e3) for i in range(EXTRA)]

    @pl.when(center)
    def _():
        for copy in copies():
            copy.wait()

        def step(i, array, row, slot, count):
            def body(t, _):
                target = table[i, t + slot]

                @pl.when(target > 0)
                def _():
                    sums[target - 1] += tiles[array, t + row].astype(F32)

                return 0

            lax.fori_loop(0, count, body, 0)

        step(4, 0, 0, 0, CAP)
        for array, pieces in enumerate(parts):
            for origin, row, slot, count in pieces:
                step(4 + origin, array + 1, row, slot, count)

    worst = functools.reduce(jnp.maximum, [m[7] for m in metas])
    for n, e in enumerate((e0, e1, e2, e3)):
        for i in range(EXTRA):
            m = metas[n * EXTRA + i]

            @pl.when((m[0] > 0) & (m[6] == r))
            def _(e=e, i=i, m=m):
                rows = slice(odd * TILE, (odd + 1) * TILE)
                sums[m[4] * LANES + m[5]] += e[i, rows, :].astype(F32)

    for t in range(CAP):
        mine[t] = sums[q * LANES + t].astype(BF)
        theirs[t] = sums[(1 - q) * LANES + t].astype(BF)
    theirs[CAP] = jnp.full((TILE, TILE), worst.astype(F32)).astype(BF)
    flag[0, 0] = worst


def final_kernel(odd, parts, where, own, atoms, table, low, left, s1, s2, s3, s4, b1, b2, b3,
                 mine, theirs, own_flag, ham, out, flag, tile, sems):
    q, r, z, y = where[0], where[1], where[2], where[3]
    kind = (r - z + SPAN) % SPAN
    for t in range(CAP):
        code = jnp.maximum(table[3, t] - 1, 0)
        d, m = code // LANES, jnp.minimum(code % LANES, CAP - 1)

        @pl.when(d == 0)
        def _(t=t, m=m):
            copy_left(kind, m, parts, left, (s1, s2, s3, s4), tile.at[t], sems.at[t])

        for i, buffer in enumerate((b1, b2, b3)):

            @pl.when(d == i + 1)
            def _(t=t, m=m, buffer=buffer):
                at = jnp.minimum(m, LIST - 1)
                pltpu.make_async_copy(buffer.at[at], tile.at[t], sems.at[t]).start()

    rows = lax.broadcasted_iota(I32, (TILE, TILE), 0)
    lanes = lax.broadcasted_iota(I32, (TILE, TILE), 1)
    diagonal = rows == lanes
    for t in range(CAP):
        pltpu.make_async_copy(left.at[0], tile.at[t], sems.at[t]).wait()
    for t in range(CAP):
        a, b = own[2 * q, t], own[2 * q + 1, t]
        total = jnp.where(table[3, t] > 0, contract(tile[t], low[t]), 0.0)
        total = total + (mine[t].astype(F32) + theirs[t].astype(F32))
        if odd:
            taken = ham[t].astype(F32)
        else:
            col = (b // 24 * SPAN + z) * RB + y * 24 + b % 24
            on = (q * SPAN + r) * RB + a == col
            functions = jnp.where(on, FUNCS * atoms[jnp.maximum(a, 0)], 0)
            taken = one(diagonal & (lanes < functions))
        out[t] = jnp.where(a >= 0, 2.0 * total - taken, 0.0).astype(BF)
    flag[0, 0] = jnp.maximum(jnp.max(theirs[CAP, :16, :].astype(F32)).astype(I32), own_flag[0, 0])


def call(kernel, outs, ins, out_specs=None, scratch=(), name=None):
    return pl.pallas_call(
        kernel,
        out_shape=outs,
        in_specs=ins,
        out_specs=out_specs if out_specs is not None else jax.tree.map(lambda _: VM, outs),
        scratch_shapes=list(scratch),
        compiler_params=pltpu.CompilerParams(vmem_limit_bytes=LIMIT),
        name=name,
        cost_estimate=pl.CostEstimate(flops=1, bytes_accessed=1, transcendentals=0),
    )


def plane(move):
    pairs = []
    for x in range(SPAN):
        for z in range(SPAN):
            to = move((x - z) % SPAN, x, z)
            if to is not None:
                for y in range(SPAN):
                    pairs.append(((x * SPAN + z) * SPAN + y, ((to[0] % SPAN) * SPAN + to[1] % SPAN) * SPAN + y))
    return pairs


RING1 = plane(lambda k, x, z: ((x, z + 1), (z, z), (z + 1, z), (x, z + 1))[k])
RING2 = plane(lambda k, x, z: ((x, z - 1), (x, z - 1), (z - 1, z), (z, z))[k])


def along_z(d):
    return [(z * SPAN + y, (z + d) % SPAN * SPAN + y) for z in range(SPAN) for y in range(SPAN)]


def along_y(d):
    return [(z * SPAN + y, z * SPAN + (y + d) % SPAN) for z in range(SPAN) for y in range(SPAN)]


def along_x(d):
    return [(x, (x + d) % SPAN) for x in range(SPAN)]


def after(value, *others):
    return lax.optimization_barrier((value, *others))[0]


def gathered(named):
    for axis, along in (("row", along_x), ("col", along_z)):
        named = jnp.concatenate([named] + [lax.ppermute(named, axis, along(d)) for d in (1, 2, 3)])
    return [named] + [lax.ppermute(named, "col", along_y(d)) for d in (1, 2, 3)]


def sparse(hamiltonian, cheb_low, cheb_high, pattern, atoms):
    shape = jax.ShapeDtypeStruct
    tiles = (CAP, TILE, TILE)
    low = cheb_low.reshape(tiles)
    high = cheb_high.reshape(tiles)
    ham = hamiltonian.reshape(tiles)
    layer, x, col = (lax.axis_index(a) for a in ("layer", "row", "col"))
    where = jnp.stack([layer, x, col // SPAN, col % SPAN]).astype(I32)
    own = pattern.reshape(4, CAP)
    a, b = pattern[:, 0, 0, 0, :], pattern[:, 0, 0, 1, :]
    k = (jnp.arange(2, dtype=I32)[:, None] * SPAN + x) * RB + a
    j = (b // 24 * SPAN + col // SPAN) * RB + col % SPAN * 24 + b % 24
    live = (a >= 0)[:, None, :]
    named = jnp.where(live, jnp.stack([k, j], axis=1), -1).astype(F32)
    named = jnp.pad(named, ((0, 0), (0, 0), (0, LANES - CAP)), constant_values=-1.0)
    patterns = gathered(named.reshape(1, 4 * LANES))

    axes = ("row", "col")
    square = call(square_kernel, (shape(tiles, BF),) * 2, [SM, VM, VM], name="square")
    even, send = square(where, low, low)
    send = after(send, patterns[0])
    p1, p2 = lax.ppermute(send, axes, RING1), lax.ppermute(send, axes, RING2)

    blob = shape((EXTRA, BLOB, TILE), BF)
    table, extra = call(
        plan_kernel, (shape((8, TILE), I32), blob), [SM, SM] + [VM] * 4 + [HB] * 2,
        scratch=[pltpu.VMEM((64, TILE), F32), pltpu.SemaphoreType.DMA((2 * EXTRA,))], name="plan",
    )(where, own, *patterns, low, high)
    odd, send = square(where, after(high, table), low)
    arrived = [lax.ppermute(extra, "col", along_z(d)) for d in (1, 2, 3)]
    send = after(send, *arrived)
    m1 = lax.ppermute(jnp.concatenate([send[:HALF], p1[:HALF]]), axes, RING1)
    m2 = lax.ppermute(jnp.concatenate([send[HALF:], p2[HALF:]]), axes, RING2)
    forward = call(forward_kernel, (blob,) * 4, [SM] + [VM] * 4, name="forward")(where, extra, *arrived)
    arrived = [lax.ppermute(forward[d], "col", along_y(d)) for d in (1, 2, 3)]
    result = call(extra_kernel, blob, [SM, SM] + [VM] * 5, name="extra")(where, own, low, forward[0], *arrived)
    entries = [result] + [lax.ppermute(result, "row", along_x(d)) for d in (1, 2, 3)]
    send = after(send, *entries)
    n1 = lax.ppermute(jnp.concatenate([send[HALF:], m1[:HALF]]), axes, RING1)
    n2 = lax.ppermute(jnp.concatenate([send[:HALF], m2[:REST]]), axes, RING2)

    lists = shape((LIST, TILE, TILE), BF)
    spreads = (p1, p2, m1, m2), (m1, m2, n1, n2)
    parts = LOW_PARTS, HIGH_PARTS
    lines, sums = [], []
    for odd_one, (left, product) in enumerate(((low, even), (high, odd))):
        packed = call(
            functools.partial(pack_kernel, parts[odd_one]), (lists,) * 3, [SM, SM] + [HB] * 5,
            scratch=[pltpu.SemaphoreType.DMA((3 * LIST,))], name="pack",
        )(where, table, left, *spreads[odd_one])
        if odd_one:
            packed = lax.optimization_barrier((*packed, *lines[0]))[:3]
        lines.append([lax.ppermute(packed[d - 1], "col", along_y(d)) for d in (1, 2, 3)])
        mine, theirs, flag = call(
            functools.partial(collect_kernel, odd_one, parts[odd_one]),
            (shape(tiles, BF), shape((CAP + 1, TILE, TILE), BF), shape((1, 1), I32)),
            [SM, SM] + [HB] * 5 + [VM] * 4,
            out_specs=(VM, VM, SM),
            scratch=[
                pltpu.VMEM((2 * LANES, TILE, TILE), F32),
                pltpu.VMEM((5, CAP + 1, TILE, TILE), BF),
                pltpu.SemaphoreType.DMA((5,)),
            ],
            name="collect",
        )(where, table, after(product, packed[0]), *spreads[odd_one], *entries)
        there = lax.ppermute(theirs, "layer", [(0, 1), (1, 0)])
        sums.append((mine, there, flag))
    results = []
    for odd_one, left in enumerate((low, high)):
        mine, there, flag = sums[odd_one]
        if not odd_one:
            mine = after(mine, sums[1][2])
        out, flag = call(
            functools.partial(final_kernel, odd_one, parts[odd_one]),
            (shape(tiles, BF), shape((1, 1), I32)),
            [SM] * 4 + [VM] + [HB] * 8 + [VM, VM, SM, VM if odd_one else HB],
            out_specs=(VM, SM),
            scratch=[pltpu.VMEM(tiles, BF), pltpu.SemaphoreType.DMA((CAP,))],
            name="finish",
        )(where, own, atoms, table, low, left, *spreads[odd_one], *lines[odd_one], mine, there, flag, ham)
        results.append(out)
    return flag, [out[None, None] for out in results]


def along(array, axis, pairs, here):
    parts = jnp.stack([array] + [lax.ppermute(array, axis, pairs(d)) for d in (1, 2, 3)])
    return jnp.take(parts, (here - jnp.arange(SPAN)) % SPAN, axis=0)


def from_center(array, x, z):
    total = jnp.where(x == z, array, jnp.zeros_like(array))
    for d in (1, 2, 3):
        pairs = plane(lambda k, a, c, d=d: (a, c + d) if k == 0 else None)
        total = total + lax.ppermute(array, ("row", "col"), pairs)
    return total


def layer_sum(sums, layer):
    halves = sums.astype(BF).reshape(2, CAP, TILE, TILE)
    kept = lax.dynamic_index_in_dim(halves, layer, 0, keepdims=False)
    sent = lax.dynamic_index_in_dim(halves, 1 - layer, 0, keepdims=False)
    got = lax.ppermute(sent, "layer", [(0, 1), (1, 0)])
    return kept.astype(F32) + got.astype(F32)


def rank_in_row(row_ids):
    earlier = jnp.arange(row_ids.shape[-1], dtype=jnp.int32)
    matches = (row_ids[..., :, None] == row_ids[..., None, :]) & (
        earlier[None, :] < earlier[:, None]
    )
    return jnp.sum(matches.astype(jnp.int32), axis=-1)


def panels(hamiltonian, cheb_low, cheb_high, pattern, atoms):
    block_rows = atoms.shape[0]
    capacity = pattern.shape[-1]
    tile_size = cheb_low.shape[-1]
    grid_rows = lax.axis_size("row")
    grid_cols = lax.axis_size("col")
    layer_count = lax.axis_size("layer")
    spread = grid_cols // grid_rows
    sub_rows = block_rows // spread
    col_width = layer_count * sub_rows
    row_index = lax.axis_index("row")
    col_index = lax.axis_index("col")
    layer_index = lax.axis_index("layer")
    own_pattern = lax.dynamic_index_in_dim(pattern[:, 0, 0], layer_index, 0, keepdims=True)[:, None]
    z, y = col_index // spread, col_index % spread
    low_panel, high_panel, index_panel = (
        along(array[0], "row", along_x, row_index) for array in (cheb_low, cheb_high, own_pattern)
    )
    low_left, high_left, index_left = (
        along(from_center(panel[:, 0], row_index, z), "col", along_y, y)
        for panel in (low_panel, high_panel, index_panel)
    )
    index_left = jnp.swapaxes(index_left, 0, 1)
    right_rows = index_panel[:, 0, 0, :]
    right_cols = index_panel[:, 0, 1, :]
    right_live = right_rows >= 0
    right_rank = rank_in_row(right_rows)
    right_count = grid_rows * capacity
    piece_ids = jnp.arange(grid_rows, dtype=jnp.int32)[:, None]
    tile_ids = piece_ids * capacity + jnp.arange(capacity, dtype=jnp.int32)[None, :]
    safe_rows = jnp.where(right_live, right_rows, block_rows)
    right_table = jnp.full((grid_rows, block_rows, SK), right_count, jnp.int32)
    right_table = right_table.at[piece_ids, safe_rows, right_rank].set(tile_ids, mode="drop")
    right_table = right_table.reshape(grid_rows * block_rows, SK)
    right_flat = low_panel.reshape(right_count, tile_size, tile_size)
    right_cols_flat = right_cols.reshape(right_count)
    out_rows = pattern[:, 0, 0, 0, :]
    out_cols = pattern[:, 0, 0, 1, :]
    layer_ids = jnp.arange(layer_count, dtype=jnp.int32)[:, None]
    out_local = jnp.where(
        out_rows >= 0, layer_ids * block_rows + out_rows, layer_count * block_rows
    )
    slot_total = layer_count * capacity
    slot_ids = layer_ids * capacity + jnp.arange(capacity, dtype=jnp.int32)[None, :]
    slot_table = jnp.full((layer_count * block_rows, col_width), slot_total, jnp.int32)
    slot_table = slot_table.at[out_local, out_cols].set(slot_ids, mode="drop")
    left_rows = index_left[:, :, 0, :]
    left_cols = index_left[:, :, 1, :]
    left_live = left_rows >= 0
    spread_ids = jnp.arange(spread, dtype=jnp.int32)[None, :, None]
    left_piece = jnp.arange(grid_rows, dtype=jnp.int32)[:, None, None]
    inner_rows = left_piece * block_rows + jnp.clip(left_rows, 0, block_rows - 1)
    target_rows = left_cols // sub_rows * block_rows + spread_ids * sub_rows + left_cols % sub_rows
    target_rows = jnp.where(left_live, target_rows, 0)
    even_sum = jnp.zeros((slot_total, tile_size, tile_size), jnp.float32)
    odd_sum = jnp.zeros((slot_total, tile_size, tile_size), jnp.float32)
    for offset in range(spread):
        block_inner = inner_rows[:, offset].reshape(-1)
        block_target = target_rows[:, offset].reshape(-1)
        block_valid = left_live[:, offset].reshape(-1)
        low_tiles = low_left[offset].reshape(-1, tile_size, tile_size)
        high_tiles = high_left[offset].reshape(-1, tile_size, tile_size)
        picked = right_table[block_inner, 0]
        usable = block_valid & (picked < right_count)
        picked = jnp.minimum(picked, right_count - 1)
        target = jnp.where(
            usable, slot_table[block_target, jnp.maximum(right_cols_flat[picked], 0)], slot_total
        )
        right_tiles = right_flat[picked]
        even_sum = even_sum.at[target].add(
            jnp.einsum("npx,npy->nxy", low_tiles, right_tiles, preferred_element_type=jnp.float32),
            mode="drop",
        )
        odd_sum = odd_sum.at[target].add(
            jnp.einsum("npx,npy->nxy", high_tiles, right_tiles, preferred_element_type=jnp.float32),
            mode="drop",
        )
    even_total, odd_total = layer_sum(even_sum, layer_index), layer_sum(odd_sum, layer_index)
    own_rows = own_pattern[0, 0, 0, :]
    own_cols = own_pattern[0, 0, 1, :]
    own_live = own_rows >= 0
    global_row = (layer_index * grid_rows + row_index) * block_rows + own_rows
    global_col = (
        (own_cols // sub_rows * grid_rows + col_index // spread) * block_rows
        + col_index % spread * sub_rows
        + own_cols % sub_rows
    )
    on_diagonal = own_live & (global_row == global_col)
    functions = FUNCS * atoms[jnp.clip(own_rows, 0, block_rows - 1)]
    across = jnp.arange(tile_size, dtype=jnp.int32)
    identity = (across[:, None] == across[None, :]) & (
        across[None, None, :] < functions[:, None, None]
    )
    identity = jnp.where(on_diagonal[:, None, None] & identity, 1.0, 0.0).astype(jnp.float32)
    live_tiles = own_live[:, None, None]
    result_even = jnp.where(live_tiles, 2.0 * even_total - identity, 0.0).astype(jnp.bfloat16)
    result_odd = jnp.where(
        live_tiles, 2.0 * odd_total - hamiltonian[0, 0].astype(jnp.float32), 0.0
    ).astype(jnp.bfloat16)
    return (result_even[None, None], result_odd[None, None])


def shards(hamiltonian, cheb_low, cheb_high, pattern, atoms):
    flag, (even, odd) = sparse(hamiltonian, cheb_low, cheb_high, pattern, atoms)
    return lax.cond(
        flag[0, 0] > 0,
        lambda: panels(hamiltonian, cheb_low, cheb_high, pattern, atoms),
        lambda: (even, odd),
    )


def solution(mesh):
    return jax.shard_map(
        shards,
        mesh=mesh,
        in_specs=(
            P(("layer", "row"), "col", None, None, None),
            P(("layer", "row"), "col", None, None, None),
            P(("layer", "row"), "col", None, None, None),
            P(None, "row", "col", None, None),
            P(("layer", "row")),
        ),
        out_specs=(
            P(("layer", "row"), "col", None, None, None),
            P(("layer", "row"), "col", None, None, None),
        ),
        check_vma=False,
    )
```

```python
import functools

import jax
import jax.numpy as jnp
from jax import lax
from jax.experimental import pallas as pl
from jax.experimental.pallas import tpu as pltpu
from jax.sharding import PartitionSpec as P

FUNCS = 8
SK = 1
TILE = 128
CAP = 23
RB = 96
LANES = 32
SPAN = 4
HALF = 12
LIST = 10
EXTRA = 2
BLOB = 2 * TILE + 16
BF = jnp.bfloat16
F32 = jnp.float32
I32 = jnp.int32
VM = pl.BlockSpec(memory_space=pltpu.VMEM)
SM = pl.BlockSpec(memory_space=pltpu.SMEM)
HB = pl.BlockSpec(memory_space=pl.ANY)
LIMIT = 56 * 1024 * 1024


def to_column(row, n):
    eye = lax.broadcasted_iota(I32, (n, n), 0) == lax.broadcasted_iota(I32, (n, n), 1)
    return jnp.sum(jnp.where(eye, row, 0.0), axis=1, keepdims=True)


def one(cond):
    return jnp.where(cond, 1.0, 0.0)


def piece_row(patterns, index, layer):
    both = patterns[pl.ds(index, 1), :]
    here = jnp.where(layer == 0, both[:, : 2 * LANES], both[:, 2 * LANES :])
    return here[:, :LANES], here[:, LANES:]


def positions(needed):
    rows = lax.broadcasted_iota(I32, (LANES, LANES), 0)
    lanes = lax.broadcasted_iota(I32, (LANES, LANES), 1)
    as_row = jnp.sum(jnp.where(rows == lanes, needed, 0.0), axis=0, keepdims=True)
    return jnp.sum(jnp.where(lanes < rows, as_row, 0.0), axis=1, keepdims=True)


def meta_block(fields):
    lanes = lax.broadcasted_iota(I32, (16, TILE), 1)
    block = jnp.zeros((16, TILE), F32)
    for i, value in enumerate(fields):
        block = jnp.where(lanes == i, value.astype(F32), block)
    return block.astype(BF)


BITS = (0, 1, 3, 5, 12, 13, 18, 20)
WIDE = (1, 2, 2, 7, 1, 5, 2, 1)


def read_meta(block):
    lanes = lax.broadcasted_iota(I32, (16, TILE), 1)
    weights = jnp.zeros((16, TILE), F32)
    for i, bit in enumerate(BITS):
        weights = jnp.where(lanes == i, float(1 << bit), weights)
    code = jnp.max(jnp.sum(block.astype(F32) * weights, axis=1, keepdims=True)).astype(I32)
    return [(code >> bit) & ((1 << wide) - 1) for bit, wide in zip(BITS, WIDE)]


def plan_kernel(where, own, g0, g1, g2, g3, low, high, table, extra, patterns, sems):
    q, r, z, y = where[0], where[1], where[2], where[3]
    for d, rows in enumerate((g0, g1, g2, g3)):
        patterns[16 * d : 16 * (d + 1), :] = rows[...]

    def row(to_x, to_z, to_y):
        dx, dz, dy = ((a - b + SPAN) % SPAN for a, b in ((r, to_x), (z, to_z), (y, to_y)))
        return dy * 16 + dz * SPAN + dx

    own_k, own_j = piece_row(patterns, 0, q)
    k_col, j_col = to_column(own_k, LANES), to_column(own_j, LANES)
    lanes = lax.broadcasted_iota(I32, (LANES, LANES), 1)
    slot_col = lax.broadcasted_iota(I32, (LANES, 1), 0).astype(F32)

    def center(s):
        ck, cj = piece_row(patterns, row(r, r, s), q)
        ck = jnp.where((ck >= 0) & (ck == cj), ck, -2.0)
        return to_column(ck, LANES)

    def needed_by(center_col, line_y):
        lk, lj = piece_row(patterns, row(r, z, line_y), q)
        lk = jnp.where(lk == lj, -1.0, lk)
        return jnp.max(one(center_col == lk), axis=1, keepdims=True)

    table[...] = jnp.zeros_like(table)
    overflow = jnp.zeros((1, 1), F32)
    mine = center(y)
    for d in range(1, SPAN):
        needed = needed_by(mine, (y + d) % SPAN)
        pos = positions(needed)
        chosen = (needed > 0) & (pos.astype(I32) == lanes)
        entries = jnp.sum(jnp.where(chosen, slot_col, 0.0), axis=0, keepdims=True)
        table[d - 1 : d, :LANES] = entries.astype(I32)
        total = jnp.sum(needed, axis=0, keepdims=True)
        overflow = jnp.maximum(overflow, one(total > LIST))
    code = jnp.zeros((1, LANES), F32)
    own_off = jnp.where(own_k == own_j, -1.0, own_k)
    for d in range(SPAN):
        there = center((y + SPAN - d) % SPAN)
        needed = needed_by(there, y)
        if d:
            entry = 1.0 + LANES * d + positions(needed)
        else:
            entry = 1.0 + slot_col
        code = code + jnp.sum(jnp.where(there == own_off, entry, 0.0), axis=0, keepdims=True)
    table[3:4, :LANES] = code.astype(I32)

    outs = []
    for layer in range(2):
        ok, oj = piece_row(patterns, row(z, z, y), layer)
        outs.append(to_column(jnp.where(ok == oj, ok, -2.0), LANES))
    for i, step in enumerate((0, 1, 3, 2)):
        _, sj = piece_row(patterns, row((z + step) % SPAN, z, y), q)
        target = jnp.zeros((1, LANES), F32)
        for layer in range(2):
            hit = (outs[layer] == sj) & (sj >= 0)
            target = target + jnp.sum(
                jnp.where(hit, 1.0 + LANES * layer + slot_col, 0.0), axis=0, keepdims=True
            )
        target = jnp.where(r == z, target, 0.0)
        table[4 + i : 5 + i, :LANES] = target.astype(I32)

    wide = lax.broadcasted_iota(I32, (LANES, 2 * LANES), 1)
    deep = lax.broadcasted_iota(I32, (LANES, 2 * LANES), 0)
    first = jnp.zeros((LANES, 2 * LANES), F32)
    second = jnp.zeros((LANES, 2 * LANES), F32)
    lefts = jnp.zeros((LANES, 2 * LANES), F32)
    rights = jnp.zeros((LANES, 2 * LANES), F32)

    def out_rows(row):
        ks = jnp.concatenate([row[:, :LANES], row[:, 2 * LANES : 3 * LANES]], axis=1)
        js = jnp.concatenate([row[:, LANES : 2 * LANES], row[:, 3 * LANES :]], axis=1)
        return ks, js

    for other in range(16):
        uk, uj = piece_row(patterns, row(r, other // SPAN, other % SPAN), q)
        partner = jnp.sum(jnp.where((k_col == uk) & (uk >= 0), uj + 1.0, 0.0), axis=1, keepdims=True) - 1.0
        vk, vj = out_rows(patterns[pl.ds(row(z, other // SPAN, other % SPAN), 1), :])
        hit = (partner == vj) & (vk == j_col) & (vk >= 0)
        hit = hit & (partner != j_col) & (j_col != k_col)
        lefts = lefts + one(hit)
        entry = jnp.where(hit, (1 + deep + LANES * wide + 2048 * other).astype(F32), 0.0)
        second = jnp.maximum(second, jnp.minimum(first, entry))
        first = jnp.maximum(first, entry)
        wk, wj = out_rows(patterns[pl.ds(row(other // SPAN, z, y), 1), :])
        hit = (partner == wk) & (wj == j_col) & (wj >= 0)
        hit = hit & (partner != j_col) & (partner != k_col)
        rights = rights + one(hit)
    many = jnp.maximum(one(jnp.sum(lefts) > EXTRA), one(jnp.sum(rights) > EXTRA))
    flag = jnp.maximum(jnp.max(overflow), many)
    top = jnp.max(first)
    next_top = jnp.maximum(jnp.max(jnp.where(first == top, 0.0, first)), jnp.max(second))
    for i, best in enumerate((top, next_top)):
        entry = best.astype(I32)
        valid = jnp.minimum(entry, 1)
        entry = jnp.maximum(entry - 1, 0)
        left = entry % LANES
        out = (entry // LANES) % (2 * LANES)
        dest = entry // 2048
        left = jnp.minimum(left, CAP - 1)
        at_row = jnp.maximum(own[2 * q, left], 0)
        for half, tiles in enumerate((low, high)):
            to = extra.at[i, pl.ds(half * TILE, TILE), :]
            pltpu.make_async_copy(tiles.at[left], to, sems.at[2 * i + half]).start()
        extra[i, 2 * TILE :, :] = meta_block(
            (valid, dest // SPAN, dest % SPAN, at_row, out // LANES, out % LANES, z, flag)
        )
    for i in range(EXTRA):
        for half, tiles in enumerate((low, high)):
            to = extra.at[i, pl.ds(half * TILE, TILE), :]
            pltpu.make_async_copy(tiles.at[0], to, sems.at[2 * i + half]).wait()


REST = CAP - HALF
LOW_PARTS = (((1, 0, 0, CAP),), ((2, 0, 0, CAP),), ((3, HALF, 0, HALF),), ((3, REST, HALF, REST),))
HIGH_PARTS = (
    ((1, 0, 0, HALF),),
    ((2, 0, HALF, REST),),
    ((1, 0, HALF, REST), (3, REST, 0, HALF)),
    ((2, 0, 0, HALF), (3, HALF, HALF, REST)),
)
FROM_CENTER = {1: 2, 2: 3, 3: 1}


def copy_left(kind, m, parts, own, spread, to, sem):
    @pl.when(kind == 0)
    def _():
        pltpu.make_async_copy(own.at[m], to, sem).start()

    for other, source in FROM_CENTER.items():
        for array, pieces in zip(spread, parts):
            for origin, row, slot, count in pieces:
                if origin == source:

                    @pl.when((kind == other) & (m >= slot) & (m < slot + count))
                    def _(array=array, row=row, slot=slot, count=count):
                        at = row + jnp.clip(m - slot, 0, count - 1)
                        pltpu.make_async_copy(array.at[at], to, sem).start()


def pack_kernel(parts, where, table, own, s1, s2, s3, s4, b1, b2, b3, sems):
    kind = (where[1] - where[2] + SPAN) % SPAN
    for d, buffer in enumerate((b1, b2, b3)):
        for j in range(LIST):
            m = jnp.minimum(table[d, j], CAP - 1)
            copy_left(kind, m, parts, own, (s1, s2, s3, s4), buffer.at[j], sems.at[d * LIST + j])
    for d, buffer in enumerate((b1, b2, b3)):
        for j in range(LIST):
            pltpu.make_async_copy(own.at[0], buffer.at[j], sems.at[d * LIST + j]).wait()


def forward_kernel(where, e0, e1, e2, e3, b0, b1, b2, b3):
    z, y = where[2], where[3]
    metas = [read_meta(e[i, 2 * TILE :, :]) for e in (e0, e1, e2, e3) for i in range(EXTRA)]
    flag = functools.reduce(jnp.maximum, [m[7] for m in metas])
    zero = jnp.int32(0)
    for d, buffer in enumerate((b0, b1, b2, b3)):
        for i in range(EXTRA):
            buffer[i] = jnp.zeros((BLOB, TILE), BF)
            buffer[i, 2 * TILE :, :] = meta_block((zero,) * 7 + (flag,))
        count = jnp.int32(0)
        for n, e in enumerate((e0, e1, e2, e3)):
            for i in range(EXTRA):
                m = metas[n * EXTRA + i]
                take = (m[0] > 0) & (m[1] == z) & (m[2] == (y + d) % SPAN)

                @pl.when(take & (count < EXTRA))
                def _(buffer=buffer, e=e, i=i, m=m, count=count):
                    buffer[count, : 2 * TILE, :] = e[i, : 2 * TILE, :]
                    buffer[count, 2 * TILE :, :] = meta_block((*m[:7], flag))

                count = count + take.astype(I32)


def contract(left, right):
    return lax.dot_general(left, right, (((0,), (0,)), ((), ())), preferred_element_type=F32)


def extra_kernel(where, own, low, e0, e1, e2, e3, result):
    q = where[0]
    metas = [read_meta(e[i, 2 * TILE :, :]) for e in (e0, e1, e2, e3) for i in range(EXTRA)]
    flag = functools.reduce(jnp.maximum, [m[7] for m in metas])
    zero = jnp.int32(0)
    for i in range(EXTRA):
        result[i] = jnp.zeros((BLOB, TILE), BF)
        result[i, 2 * TILE :, :] = meta_block((zero,) * 7 + (flag,))
    count = jnp.int32(0)
    for n, e in enumerate((e0, e1, e2, e3)):
        for i in range(EXTRA):
            m = metas[n * EXTRA + i]
            take = m[0] > 0

            @pl.when(take & (count < EXTRA))
            def _(e=e, i=i, m=m, count=count):
                def find(t, at):
                    return jnp.where(own[2 * q, t] == m[3], t, at)

                right = low[lax.fori_loop(0, CAP, find, jnp.int32(0))]
                for half in range(2):
                    rows = slice(half * TILE, (half + 1) * TILE)
                    result[count, rows, :] = contract(e[i, rows, :], right).astype(BF)
                result[count, 2 * TILE :, :] = meta_block((*m[:7], flag))

            count = count + take.astype(I32)


def square_kernel(where, left, low, product, send):
    center = where[1] == where[2]
    for t in range(CAP):
        product[t] = contract(left[t], low[t]).astype(BF)

    @pl.when(center)
    def _():
        send[...] = left[...]

    @pl.when(jnp.logical_not(center))
    def _():
        send[...] = product[...]


def collect_kernel(odd, parts, where, table, own, s1, s2, s3, s4, e0, e1, e2, e3,
                   mine, theirs, more, flag, sums, tiles, sems):
    q, r = where[0], where[1]
    center = r == where[2]
    sources = (own, s1, s2, s3, s4)

    def copies():
        return [
            pltpu.make_async_copy(array, tiles.at[i, pl.ds(0, array.shape[0])], sems.at[i])
            for i, array in enumerate(sources)
        ]

    @pl.when(center)
    def _():
        for copy in copies():
            copy.start()

    sums[...] = jnp.zeros_like(sums)
    metas = [read_meta(e[i, 2 * TILE :, :]) for e in (e0, e1, e2, e3) for i in range(EXTRA)]

    @pl.when(center)
    def _():
        for copy in copies():
            copy.wait()

        def step(i, array, row, slot, count):
            for t in range(count):
                target = table[i, t + slot]
                target = jnp.where(target > 0, target - 1, 2 * LANES - 1)
                sums[target] += tiles[array, t + row].astype(F32)

        step(4, 0, 0, 0, CAP)
        for array, pieces in enumerate(parts):
            for origin, row, slot, count in pieces:
                step(4 + origin, array + 1, row, slot, count)

    worst = functools.reduce(jnp.maximum, [m[7] for m in metas])
    for n, e in enumerate((e0, e1, e2, e3)):
        for i in range(EXTRA):
            m = metas[n * EXTRA + i]

            @pl.when((m[0] > 0) & (m[6] == r))
            def _(e=e, i=i, m=m):
                rows = slice(odd * TILE, (odd + 1) * TILE)
                sums[m[4] * LANES + m[5]] += e[i, rows, :].astype(F32)

    for t in range(CAP):
        mine[t] = sums[q * LANES + t].astype(BF)
        to, at = (theirs, t) if t < HALF else (more, t - HALF)
        to[at] = sums[(1 - q) * LANES + t].astype(BF)
    more[REST] = jnp.full((TILE, TILE), worst.astype(F32)).astype(BF)
    flag[0, 0] = worst


def final_kernel(odd, parts, where, own, atoms, table, low, left, s1, s2, s3, s4, b1, b2, b3,
                 mine, theirs, more, own_flag, ham, out, flag, tile, sems):
    q, r, z, y = where[0], where[1], where[2], where[3]
    kind = (r - z + SPAN) % SPAN
    for t in range(CAP):
        code = jnp.maximum(table[3, t] - 1, 0)
        d, m = code // LANES, jnp.minimum(code % LANES, CAP - 1)

        @pl.when(d == 0)
        def _(t=t, m=m):
            copy_left(kind, m, parts, left, (s1, s2, s3, s4), tile.at[t], sems.at[t])

        for i, buffer in enumerate((b1, b2, b3)):

            @pl.when(d == i + 1)
            def _(t=t, m=m, buffer=buffer):
                at = jnp.minimum(m, LIST - 1)
                pltpu.make_async_copy(buffer.at[at], tile.at[t], sems.at[t]).start()

    rows = lax.broadcasted_iota(I32, (TILE, TILE), 0)
    lanes = lax.broadcasted_iota(I32, (TILE, TILE), 1)
    diagonal = rows == lanes
    for t in range(CAP):
        pltpu.make_async_copy(left.at[0], tile.at[t], sems.at[t]).wait()
    for t in range(CAP):
        a, b = own[2 * q, t], own[2 * q + 1, t]
        total = jnp.where(table[3, t] > 0, contract(tile[t], low[t]), 0.0)
        crossed = theirs[t] if t < HALF else more[t - HALF]
        total = total + (mine[t].astype(F32) + crossed.astype(F32))
        if odd:
            taken = ham[t].astype(F32)
        else:
            col = (b // 24 * SPAN + z) * RB + y * 24 + b % 24
            on = (q * SPAN + r) * RB + a == col
            functions = jnp.where(on, FUNCS * atoms[jnp.maximum(a, 0)], 0)
            taken = one(diagonal & (lanes < functions))
        out[t] = jnp.where(a >= 0, 2.0 * total - taken, 0.0).astype(BF)
    flag[0, 0] = jnp.maximum(jnp.max(more[REST, :16, :].astype(F32)).astype(I32), own_flag[0, 0])


def call(kernel, outs, ins, out_specs=None, scratch=(), name=None):
    return pl.pallas_call(
        kernel,
        out_shape=outs,
        in_specs=ins,
        out_specs=out_specs if out_specs is not None else jax.tree.map(lambda _: VM, outs),
        scratch_shapes=list(scratch),
        compiler_params=pltpu.CompilerParams(vmem_limit_bytes=LIMIT),
        name=name,
        cost_estimate=pl.CostEstimate(flops=1, bytes_accessed=1, transcendentals=0),
    )


def plane(move):
    pairs = []
    for x in range(SPAN):
        for z in range(SPAN):
            to = move((x - z) % SPAN, x, z)
            if to is not None:
                for y in range(SPAN):
                    pairs.append(((x * SPAN + z) * SPAN + y, ((to[0] % SPAN) * SPAN + to[1] % SPAN) * SPAN + y))
    return pairs


RING1 = plane(lambda k, x, z: ((x, z + 1), (z, z), (z + 1, z), (x, z + 1))[k])
RING2 = plane(lambda k, x, z: ((x, z - 1), (x, z - 1), (z - 1, z), (z, z))[k])


def along_z(d):
    return [(z * SPAN + y, (z + d) % SPAN * SPAN + y) for z in range(SPAN) for y in range(SPAN)]


def along_y(d):
    return [(z * SPAN + y, z * SPAN + (y + d) % SPAN) for z in range(SPAN) for y in range(SPAN)]


def along_x(d):
    return [(x, (x + d) % SPAN) for x in range(SPAN)]


def after(value, *others):
    return lax.optimization_barrier((value, *others))[0]


def gathered(named):
    for axis, along in (("row", along_x), ("col", along_z)):
        named = jnp.concatenate([named] + [lax.ppermute(named, axis, along(d)) for d in (1, 2, 3)])
    return [named] + [lax.ppermute(named, "col", along_y(d)) for d in (1, 2, 3)]


def sparse(hamiltonian, cheb_low, cheb_high, pattern, atoms):
    shape = jax.ShapeDtypeStruct
    tiles = (CAP, TILE, TILE)
    low = cheb_low.reshape(tiles)
    high = cheb_high.reshape(tiles)
    ham = hamiltonian.reshape(tiles)
    layer, x, col = (lax.axis_index(a) for a in ("layer", "row", "col"))
    where = jnp.stack([layer, x, col // SPAN, col % SPAN]).astype(I32)
    own = pattern.reshape(4, CAP)
    a, b = pattern[:, 0, 0, 0, :], pattern[:, 0, 0, 1, :]
    k = (jnp.arange(2, dtype=I32)[:, None] * SPAN + x) * RB + a
    j = (b // 24 * SPAN + col // SPAN) * RB + col % SPAN * 24 + b % 24
    live = (a >= 0)[:, None, :]
    named = jnp.where(live, jnp.stack([k, j], axis=1), -1).astype(F32)
    named = jnp.pad(named, ((0, 0), (0, 0), (0, LANES - CAP)), constant_values=-1.0)
    patterns = gathered(named.reshape(1, 4 * LANES))

    axes = ("row", "col")
    square = call(square_kernel, (shape(tiles, BF),) * 2, [SM, VM, VM], name="square")
    even, send = square(where, low, low)
    send = after(send, patterns[0])
    p1, p2 = lax.ppermute(send, axes, RING1), lax.ppermute(send, axes, RING2)

    blob = shape((EXTRA, BLOB, TILE), BF)
    table, extra = call(
        plan_kernel, (shape((8, TILE), I32), blob), [SM, SM] + [VM] * 4 + [HB] * 2,
        scratch=[pltpu.VMEM((64, TILE), F32), pltpu.SemaphoreType.DMA((2 * EXTRA,))], name="plan",
    )(where, own, *patterns, low, high)
    odd, send = square(where, after(high, table), low)
    arrived = [lax.ppermute(extra, "col", along_z(d)) for d in (1, 2, 3)]
    send = after(send, *arrived)
    m1 = lax.ppermute(jnp.concatenate([send[:HALF], p1[:HALF]]), axes, RING1)
    m2 = lax.ppermute(jnp.concatenate([send[HALF:], p2[HALF:]]), axes, RING2)
    forward = call(forward_kernel, (blob,) * 4, [SM] + [VM] * 4, name="forward")(where, extra, *arrived)
    arrived = [lax.ppermute(forward[d], "col", along_y(d)) for d in (1, 2, 3)]
    result = call(extra_kernel, blob, [SM, SM] + [VM] * 5, name="extra")(where, own, low, forward[0], *arrived)
    entries = [result] + [lax.ppermute(result, "row", along_x(d)) for d in (1, 2, 3)]
    send = after(send, *entries)
    n1 = lax.ppermute(jnp.concatenate([send[HALF:], m1[:HALF]]), axes, RING1)
    n2 = lax.ppermute(jnp.concatenate([send[:HALF], m2[:REST]]), axes, RING2)

    lists = shape((LIST, TILE, TILE), BF)
    spreads = (p1, p2, m1, m2), (m1, m2, n1, n2)
    parts = LOW_PARTS, HIGH_PARTS
    lines, sums = [], []
    for odd_one, (left, product) in enumerate(((low, even), (high, odd))):
        packed = call(
            functools.partial(pack_kernel, parts[odd_one]), (lists,) * 3, [SM, SM] + [HB] * 5,
            scratch=[pltpu.SemaphoreType.DMA((3 * LIST,))], name="pack",
        )(where, table, left, *spreads[odd_one])
        if odd_one:
            packed = lax.optimization_barrier((*packed, *lines[0]))[:3]
        lines.append([lax.ppermute(packed[d - 1], "col", along_y(d)) for d in (1, 2, 3)])
        mine, theirs, more, flag = call(
            functools.partial(collect_kernel, odd_one, parts[odd_one]),
            (shape(tiles, BF),) + (shape((HALF, TILE, TILE), BF),) * 2 + (shape((1, 1), I32),),
            [SM, SM] + [HB] * 5 + [VM] * 4,
            out_specs=(VM, VM, VM, SM),
            scratch=[
                pltpu.VMEM((2 * LANES, TILE, TILE), F32),
                pltpu.VMEM((5, CAP + 1, TILE, TILE), BF),
                pltpu.SemaphoreType.DMA((5,)),
            ],
            name="collect",
        )(where, table, after(product, packed[0]), *spreads[odd_one], *entries)
        there = [lax.ppermute(half, "layer", [(0, 1), (1, 0)]) for half in (theirs, more)]
        sums.append((mine, there, flag))
    results = []
    for odd_one, left in enumerate((low, high)):
        mine, there, flag = sums[odd_one]
        if not odd_one:
            mine = after(mine, sums[1][2])
        out, flag = call(
            functools.partial(final_kernel, odd_one, parts[odd_one]),
            (shape(tiles, BF), shape((1, 1), I32)),
            [SM] * 4 + [VM] + [HB] * 8 + [VM, VM, VM, SM, VM if odd_one else HB],
            out_specs=(VM, SM),
            scratch=[pltpu.VMEM(tiles, BF), pltpu.SemaphoreType.DMA((CAP,))],
            name="finish",
        )(where, own, atoms, table, low, left, *spreads[odd_one], *lines[odd_one], mine, *there, flag, ham)
        results.append(out)
    return flag, [out[None, None] for out in results]


def along(array, axis, pairs, here):
    parts = jnp.stack([array] + [lax.ppermute(array, axis, pairs(d)) for d in (1, 2, 3)])
    return jnp.take(parts, (here - jnp.arange(SPAN)) % SPAN, axis=0)


def from_center(array, x, z):
    total = jnp.where(x == z, array, jnp.zeros_like(array))
    for d in (1, 2, 3):
        pairs = plane(lambda k, a, c, d=d: (a, c + d) if k == 0 else None)
        total = total + lax.ppermute(array, ("row", "col"), pairs)
    return total


def layer_sum(sums, layer):
    halves = sums.astype(BF).reshape(2, CAP, TILE, TILE)
    kept = lax.dynamic_index_in_dim(halves, layer, 0, keepdims=False)
    sent = lax.dynamic_index_in_dim(halves, 1 - layer, 0, keepdims=False)
    got = lax.ppermute(sent, "layer", [(0, 1), (1, 0)])
    return kept.astype(F32) + got.astype(F32)


def rank_in_row(row_ids):
    earlier = jnp.arange(row_ids.shape[-1], dtype=jnp.int32)
    matches = (row_ids[..., :, None] == row_ids[..., None, :]) & (
        earlier[None, :] < earlier[:, None]
    )
    return jnp.sum(matches.astype(jnp.int32), axis=-1)


def panels(hamiltonian, cheb_low, cheb_high, pattern, atoms):
    block_rows = atoms.shape[0]
    capacity = pattern.shape[-1]
    tile_size = cheb_low.shape[-1]
    grid_rows = lax.axis_size("row")
    grid_cols = lax.axis_size("col")
    layer_count = lax.axis_size("layer")
    spread = grid_cols // grid_rows
    sub_rows = block_rows // spread
    col_width = layer_count * sub_rows
    row_index = lax.axis_index("row")
    col_index = lax.axis_index("col")
    layer_index = lax.axis_index("layer")
    own_pattern = lax.dynamic_index_in_dim(pattern[:, 0, 0], layer_index, 0, keepdims=True)[:, None]
    z, y = col_index // spread, col_index % spread
    low_panel, high_panel, index_panel = (
        along(array[0], "row", along_x, row_index) for array in (cheb_low, cheb_high, own_pattern)
    )
    low_left, high_left, index_left = (
        along(from_center(panel[:, 0], row_index, z), "col", along_y, y)
        for panel in (low_panel, high_panel, index_panel)
    )
    index_left = jnp.swapaxes(index_left, 0, 1)
    right_rows = index_panel[:, 0, 0, :]
    right_cols = index_panel[:, 0, 1, :]
    right_live = right_rows >= 0
    right_rank = rank_in_row(right_rows)
    right_count = grid_rows * capacity
    piece_ids = jnp.arange(grid_rows, dtype=jnp.int32)[:, None]
    tile_ids = piece_ids * capacity + jnp.arange(capacity, dtype=jnp.int32)[None, :]
    safe_rows = jnp.where(right_live, right_rows, block_rows)
    right_table = jnp.full((grid_rows, block_rows, SK), right_count, jnp.int32)
    right_table = right_table.at[piece_ids, safe_rows, right_rank].set(tile_ids, mode="drop")
    right_table = right_table.reshape(grid_rows * block_rows, SK)
    right_flat = low_panel.reshape(right_count, tile_size, tile_size)
    right_cols_flat = right_cols.reshape(right_count)
    out_rows = pattern[:, 0, 0, 0, :]
    out_cols = pattern[:, 0, 0, 1, :]
    layer_ids = jnp.arange(layer_count, dtype=jnp.int32)[:, None]
    out_local = jnp.where(
        out_rows >= 0, layer_ids * block_rows + out_rows, layer_count * block_rows
    )
    slot_total = layer_count * capacity
    slot_ids = layer_ids * capacity + jnp.arange(capacity, dtype=jnp.int32)[None, :]
    slot_table = jnp.full((layer_count * block_rows, col_width), slot_total, jnp.int32)
    slot_table = slot_table.at[out_local, out_cols].set(slot_ids, mode="drop")
    left_rows = index_left[:, :, 0, :]
    left_cols = index_left[:, :, 1, :]
    left_live = left_rows >= 0
    spread_ids = jnp.arange(spread, dtype=jnp.int32)[None, :, None]
    left_piece = jnp.arange(grid_rows, dtype=jnp.int32)[:, None, None]
    inner_rows = left_piece * block_rows + jnp.clip(left_rows, 0, block_rows - 1)
    target_rows = left_cols // sub_rows * block_rows + spread_ids * sub_rows + left_cols % sub_rows
    target_rows = jnp.where(left_live, target_rows, 0)
    even_sum = jnp.zeros((slot_total, tile_size, tile_size), jnp.float32)
    odd_sum = jnp.zeros((slot_total, tile_size, tile_size), jnp.float32)
    for offset in range(spread):
        block_inner = inner_rows[:, offset].reshape(-1)
        block_target = target_rows[:, offset].reshape(-1)
        block_valid = left_live[:, offset].reshape(-1)
        low_tiles = low_left[offset].reshape(-1, tile_size, tile_size)
        high_tiles = high_left[offset].reshape(-1, tile_size, tile_size)
        picked = right_table[block_inner, 0]
        usable = block_valid & (picked < right_count)
        picked = jnp.minimum(picked, right_count - 1)
        target = jnp.where(
            usable, slot_table[block_target, jnp.maximum(right_cols_flat[picked], 0)], slot_total
        )
        right_tiles = right_flat[picked]
        even_sum = even_sum.at[target].add(
            jnp.einsum("npx,npy->nxy", low_tiles, right_tiles, preferred_element_type=jnp.float32),
            mode="drop",
        )
        odd_sum = odd_sum.at[target].add(
            jnp.einsum("npx,npy->nxy", high_tiles, right_tiles, preferred_element_type=jnp.float32),
            mode="drop",
        )
    even_total, odd_total = layer_sum(even_sum, layer_index), layer_sum(odd_sum, layer_index)
    own_rows = own_pattern[0, 0, 0, :]
    own_cols = own_pattern[0, 0, 1, :]
    own_live = own_rows >= 0
    global_row = (layer_index * grid_rows + row_index) * block_rows + own_rows
    global_col = (
        (own_cols // sub_rows * grid_rows + col_index // spread) * block_rows
        + col_index % spread * sub_rows
        + own_cols % sub_rows
    )
    on_diagonal = own_live & (global_row == global_col)
    functions = FUNCS * atoms[jnp.clip(own_rows, 0, block_rows - 1)]
    across = jnp.arange(tile_size, dtype=jnp.int32)
    identity = (across[:, None] == across[None, :]) & (
        across[None, None, :] < functions[:, None, None]
    )
    identity = jnp.where(on_diagonal[:, None, None] & identity, 1.0, 0.0).astype(jnp.float32)
    live_tiles = own_live[:, None, None]
    result_even = jnp.where(live_tiles, 2.0 * even_total - identity, 0.0).astype(jnp.bfloat16)
    result_odd = jnp.where(
        live_tiles, 2.0 * odd_total - hamiltonian[0, 0].astype(jnp.float32), 0.0
    ).astype(jnp.bfloat16)
    return (result_even[None, None], result_odd[None, None])


def shards(hamiltonian, cheb_low, cheb_high, pattern, atoms):
    flag, (even, odd) = sparse(hamiltonian, cheb_low, cheb_high, pattern, atoms)
    return lax.cond(
        flag[0, 0] > 0,
        lambda: panels(hamiltonian, cheb_low, cheb_high, pattern, atoms),
        lambda: (even, odd),
    )


def solution(mesh):
    return jax.shard_map(
        shards,
        mesh=mesh,
        in_specs=(
            P(("layer", "row"), "col", None, None, None),
            P(("layer", "row"), "col", None, None, None),
            P(("layer", "row"), "col", None, None, None),
            P(None, "row", "col", None, None),
            P(("layer", "row")),
        ),
        out_specs=(
            P(("layer", "row"), "col", None, None, None),
            P(("layer", "row"), "col", None, None, None),
        ),
        check_vma=False,
    )
```
